256 devices in a mesh: ctx: 64 (over y, z, core), kvg: 4 (over x).
Axes of the slice: x: 4, y: 4, z: 8, core: 2. Of those that a mesh axis runs over, the one named last changes fastest.
Arguments:
- tokens: bfloat16 [8192, 4096], P('ctx', 'kvg'), may hold values from -14 to 14
- questions: bfloat16 [512, 4096], P('ctx', 'kvg'), may hold values from -14 to 14
- q_weight: bfloat16 [4096, 2048], P(None, 'kvg'), may hold values from -0.09375 to 0.09375
- k_weight: bfloat16 [4096, 512], P(None, 'kvg'), may hold values from -0.09375 to 0.09375
- v_weight: bfloat16 [4096, 512], P(None, 'kvg'), may hold values from -0.09375 to 0.09375
- o_weight: bfloat16 [2048, 4096], P('kvg'), may hold values from -0.125 to 0.125
- anchor: int32 [1], replicated, may hold values from 0 to 63
- lengths: int32 [64], replicated, may hold values from 32 to 128, as said below
- positions: int32 [512], replicated, may hold values from 0 to 8191
Outputs:
- context_out: bfloat16 [8192, 4096], P('ctx', 'kvg')
- question_out: bfloat16 [512, 4096], P('ctx', 'kvg')
The draws below stay inside these ranges and needn't reach their ends.
Inputs may be any that keep to these rules, and one draw needn't show every extreme that they name: `lengths`: every block has at least 32 valid tokens; some block is full and some block has exactly 32.
All inputs are finite; a program needn't handle non-finite values.
Results may differ from the reference program's by a relative error of at most 0.03.
Values may be sent and summed in bfloat16 or wider, within the bound.
A program may use at most 320 MiB of HBM per device.

```python
import math
import jax
import jax.numpy as jnp
from jax import lax

D = 4096
HEADS = 16
KV_HEADS = 4
HEAD_DIM = 128
BLK = 128
QDEV = 8
NBLK = 64
TOKENS = 8192
QROWS = 512
N_KVG = 4


def draw_tokens(key, part):
    key = jax.random.fold_in(key, 3)
    first_key = jax.random.fold_in(key, 0)
    values = jnp.clip(jax.random.normal(first_key, (TOKENS, D), jnp.float32), -5.0, 5.0)
    return values.astype(jnp.bfloat16)


def draw_questions(key, part):
    key = jax.random.fold_in(key, 5)
    first_key = jax.random.fold_in(key, 0)
    values = jnp.clip(jax.random.normal(first_key, (QROWS, D), jnp.float32), -5.0, 5.0)
    return values.astype(jnp.bfloat16)


def draw_lengths(key, part):
    key = jax.random.fold_in(key, 7)
    first_key, second_key, third_key = jax.random.split(key, 3)
    base_len = jax.random.randint(first_key, (NBLK,), BLK // 4, BLK + 1, dtype=jnp.int32)
    full_pick = jax.random.randint(second_key, (), 0, NBLK, dtype=jnp.int32)
    short_pick = (full_pick + 1 + jax.random.randint(third_key, (), 0, NBLK - 1, dtype=jnp.int32)) % NBLK
    indices = jnp.arange(NBLK, dtype=jnp.int32)
    base_len = jnp.where(indices == short_pick, BLK // 4, base_len)
    base_len = jnp.where(indices == full_pick, BLK, base_len)
    return base_len.astype(jnp.int32)


def plant(result, stream_key, smallest, largest):
    longest = result.shape.index(max(result.shape))
    spots = []
    for shift in (0, 1):
        where = [jax.random.randint(jax.random.fold_in(stream_key, axis), (), 0, length) for axis, length in enumerate(result.shape)]
        where[longest] = (where[longest] + shift) % result.shape[longest]
        spots.append(tuple(where))
    return result.at[spots[0]].set(smallest).at[spots[1]].set(largest)


def shard_levels(key, dims, pieces, low, top_value):
    level, own = 1.0, jax.random.fold_in(key, 6)
    for axis_at, blocks in pieces:
        draws = jnp.exp(jax.random.uniform(jax.random.fold_in(own, axis_at), (blocks,), jnp.float32, low / len(pieces), top_value / len(pieces)))
        level = level * jnp.repeat(draws, dims[axis_at] // blocks).reshape([-1 if axis == axis_at else 1 for axis in range(len(dims))])
    return level


def centred(rng, shape, spread, limit, shards=(), kind=jnp.bfloat16):
    factor_of = shard_levels(rng, shape, shards, -0.22, 0.18) if shards else 1.0
    entries = jax.random.normal(rng, shape, jnp.float32) * spread * factor_of
    return jnp.minimum(jnp.maximum(entries, -limit), limit).astype(kind)


def setup_inputs(seed: int = 0) -> dict:
    arg_keys = jax.random.split(jax.random.key(seed), 10)
    return {
        "tokens": draw_tokens(jax.random.fold_in(arg_keys[9], 71), 0),
        "questions": draw_questions(jax.random.fold_in(arg_keys[9], 71), 0),
        "q_weight": centred(arg_keys[2], (D, HEADS * HEAD_DIM), D ** -0.5, 0.09375, ((1, 4),)),
        "k_weight": centred(arg_keys[3], (D, KV_HEADS * HEAD_DIM), D ** -0.5, 0.09375, ((1, 4),)),
        "v_weight": centred(arg_keys[4], (D, KV_HEADS * HEAD_DIM), D ** -0.5, 0.09375, ((1, 4),)),
        "o_weight": centred(arg_keys[5], (HEADS * HEAD_DIM, D), (HEADS * HEAD_DIM) ** -0.5, 0.125, ((0, 4),)),
        "anchor": jax.random.randint(arg_keys[6], (1,), 0, NBLK).astype(jnp.int32),
        "lengths": draw_lengths(jax.random.fold_in(arg_keys[9], 71), 0),
        "positions": plant(jax.random.randint(arg_keys[8], (QROWS,), 0, TOKENS), jax.random.fold_in(arg_keys[8], 1), 0, TOKENS - 1).astype(jnp.int32),
    }


NEG_BIG = -1.0e30


def rotary(values, places):
    half_dim = values.shape[-1] // 2
    frequency = jnp.exp(jnp.arange(half_dim, dtype=jnp.float32) * (-2.0 * math.log(500000.0) / values.shape[-1]))
    angle = places.astype(jnp.float32)[:, None] * frequency[None, :]
    cosine = jnp.cos(angle)[:, None, :]
    sine = jnp.sin(angle)[:, None, :]
    front_part = values[..., :half_dim]
    back_part = values[..., half_dim:]
    return jnp.concatenate([front_part * cosine - back_part * sine, back_part * cosine + front_part * sine], -1)


def project_out(attended, o_weight):
    slab_width = HEADS * HEAD_DIM // N_KVG
    summed = jnp.zeros((attended.shape[0], D), jnp.float32)
    for group_index in range(N_KVG):
        lower = group_index * slab_width
        partial_term = jnp.dot(attended[:, lower:lower + slab_width], o_weight[lower:lower + slab_width], preferred_element_type=jnp.float32)
        summed = summed + lax.optimization_barrier(partial_term.astype(jnp.bfloat16)).astype(jnp.float32)
    return summed.astype(jnp.bfloat16)


def reference(tokens, questions, q_weight, k_weight, v_weight, o_weight, anchor, lengths, positions):
    groups = HEADS // KV_HEADS
    scale = HEAD_DIM ** -0.5
    places = jnp.arange(TOKENS, dtype=jnp.int32)
    query_all = rotary(jnp.dot(tokens, q_weight, preferred_element_type=jnp.float32).reshape(TOKENS, HEADS, HEAD_DIM), places)
    query_all = query_all.astype(jnp.bfloat16).reshape(TOKENS, KV_HEADS, groups, HEAD_DIM)
    key_all = rotary(jnp.dot(tokens, k_weight, preferred_element_type=jnp.float32).reshape(TOKENS, KV_HEADS, HEAD_DIM), places).astype(jnp.bfloat16)
    value_all = jnp.dot(tokens, v_weight, preferred_element_type=jnp.float32).astype(jnp.bfloat16).reshape(TOKENS, KV_HEADS, HEAD_DIM)
    anchor_index = anchor[0].astype(jnp.int32)
    anchor_keys = lax.dynamic_slice_in_dim(key_all, anchor_index * BLK, BLK, 0)
    anchor_values = lax.dynamic_slice_in_dim(value_all, anchor_index * BLK, BLK, 0)
    anchor_length = lax.dynamic_slice_in_dim(lengths, anchor_index, 1, 0)[0]
    query_pos = jnp.arange(BLK, dtype=jnp.int32)[:, None]
    key_pos = jnp.arange(2 * BLK, dtype=jnp.int32)[None, :]

    def one_block(block_index):
        own_length = lax.dynamic_slice_in_dim(lengths, block_index, 1, 0)[0]
        queries = lax.dynamic_slice_in_dim(query_all, block_index * BLK, BLK, 0)
        key_rows = jnp.concatenate([lax.dynamic_slice_in_dim(key_all, block_index * BLK, BLK, 0), anchor_keys], 0)
        value_rows = jnp.concatenate([lax.dynamic_slice_in_dim(value_all, block_index * BLK, BLK, 0), anchor_values], 0)
        own_seen = (key_pos < BLK) & (key_pos <= query_pos) & (key_pos < own_length)
        far_seen = (key_pos >= BLK) & (key_pos - BLK < anchor_length) & (block_index != anchor_index)
        visible = own_seen | far_seen
        scores = jnp.einsum('qkgd,skd->kgqs', queries.astype(jnp.float32), key_rows.astype(jnp.float32), precision=lax.Precision.HIGHEST) * scale
        row_max = jnp.max(jnp.where(visible, scores, NEG_BIG), axis=-1, keepdims=True)
        weights = jnp.where(visible, jnp.exp(scores - row_max), 0.0)
        denominator = jnp.sum(weights, axis=-1)
        rounded = lax.optimization_barrier(weights.astype(jnp.bfloat16)).astype(jnp.float32)
        numerator = jnp.einsum('kgqs,skd->qkgd', rounded, value_rows.astype(jnp.float32), precision=lax.Precision.HIGHEST)
        attended = numerator / jnp.transpose(denominator, (2, 0, 1))[..., None]
        return attended.astype(jnp.bfloat16).reshape(BLK, HEADS * HEAD_DIM)

    attention = lax.map(one_block, jnp.arange(NBLK, dtype=jnp.int32)).reshape(TOKENS, HEADS * HEAD_DIM)

    question_q = rotary(jnp.dot(questions, q_weight, preferred_element_type=jnp.float32).reshape(QROWS, HEADS, HEAD_DIM), positions)
    question_q = question_q.astype(jnp.bfloat16).reshape(NBLK, QDEV, KV_HEADS, groups, HEAD_DIM)
    question_pos = positions.reshape(NBLK, QDEV)
    key_valid = (places % BLK) < jnp.repeat(lengths, BLK)
    key_float = key_all.astype(jnp.float32)
    value_float = value_all.astype(jnp.float32)

    def one_group(packed):
        queries, reach = packed
        scores = jnp.einsum('qkgd,skd->qkgs', queries.astype(jnp.float32), key_float, precision=lax.Precision.HIGHEST) * scale
        visible = (key_valid[None, :] & (places[None, :] <= reach[:, None]))[:, None, None, :]
        row_max = jnp.max(jnp.where(visible, scores, NEG_BIG), axis=-1, keepdims=True)
        weights = jnp.where(visible, jnp.exp(scores - row_max), 0.0)
        denominator = jnp.sum(weights, axis=-1)
        numerator = jnp.einsum('qkgs,skd->qkgd', weights, value_float, precision=lax.Precision.HIGHEST)
        return (numerator / denominator[..., None]).astype(jnp.bfloat16).reshape(QDEV, HEADS * HEAD_DIM)

    question_att = lax.map(one_group, (question_q, question_pos)).reshape(QROWS, HEADS * HEAD_DIM)
    return project_out(attention, o_weight), project_out(question_att, o_weight)
```

```python
import math

import jax
import jax.numpy as jnp
from jax import lax
from jax.experimental import pallas as pl
from jax.experimental.pallas import tpu as pltpu
from jax.sharding import PartitionSpec as P

HEAD_DIM = 128
NX = 4
NY, NZ, NC = 4, 8, 2
BLK = 128
QROW = 8
HEADS = 4
FEAT = 1024
QCOLS = HEADS * HEAD_DIM
WCOLS = QCOLS + 2 * HEAD_DIM
NEG_BIG = -1e30
SCALE = HEAD_DIM ** (-0.5)
F32 = jnp.float32
BF16 = jnp.bfloat16
MESH = pl.DeviceIdType.MESH
N_COPIES = 80
N_LOADS = 17


def dot_nn(a, b):
    return jnp.dot(a, b, preferred_element_type=F32)


def dot_nt(a, b):
    return lax.dot_general(a, b, (((1,), (1,)), ((), ())), preferred_element_type=F32)


def dot_tn(a, b):
    return lax.dot_general(a, b, (((0,), (0,)), ((), ())), preferred_element_type=F32)


def angles(places):
    lane = lax.broadcasted_iota(jnp.int32, places.shape, 1)
    half = HEAD_DIM // 2
    index = jnp.where(lane < half, lane, lane - half).astype(F32)
    frequency = jnp.exp(index * (-2.0 * math.log(500000.0) / HEAD_DIM))
    angle = places.astype(F32) * frequency
    sine = jnp.sin(angle)
    return jnp.cos(angle), jnp.where(lane < half, -sine, sine)


def rotate(head, cosine, sine):
    return head * cosine + pltpu.roll(head, HEAD_DIM // 2, 1) * sine


def kernel(
    tokens, questions, wq, wk, wv, wo, anchor, lengths, positions,
    ctx_out, q_out,
    w_in, w_out, tok, qpack, acc, q4, qz, kvb, a1, a2, anc,
    part, stats, part_in, stats_in, tr_out, tr_in, to_right, to_left, from_left, from_right,
    own_term, qx_out, qx_in, load_sem, send_sem, recv_sem,
):
    n_p = NY * NC
    piece = 2 * BLK // n_p
    c = lax.axis_index("ctx")
    g = lax.axis_index("kvg")
    core = lax.rem(c, NC)
    z = lax.rem(lax.div(c, NC), NZ)
    y = lax.div(c, NC * NZ)
    p = y * NC + core

    def at(y_, z_, core_):
        return (y_ * NZ + z_) * NC + core_

    src = [g, lax.rem(g + 3, NX), lax.rem(g + 1, NX), lax.rem(g + 2, NX)]
    left, right, opposite = (c, src[1]), (c, src[2]), (c, src[3])

    def p_peer(d):
        q = lax.rem(p + d, n_p)
        return (at(lax.div(q, NC), z, lax.rem(q, NC)), g)

    def z_peer(d):
        return (at(y, lax.rem(z + d, NZ), core), g)

    def y_peer(d):
        return (at(lax.rem(y + d, NY), z, core), g)

    sibling = (at(y, z, 1 - core), g)

    loads = []

    def load(source, target):
        copy = pltpu.make_async_copy(source, target, load_sem.at[len(loads)])
        copy.start()
        loads.append(copy)
        return copy

    tok_load = load(tokens, tok.at[0])
    w_loads = []
    for slot in range(NX):
        rows = pl.ds(pl.multiple_of(src[slot] * FEAT, FEAT), FEAT)
        w_loads.append([
            load(wq.at[rows, :], w_in.at[slot, :, pl.ds(0, QCOLS)]),
            load(wk.at[rows, :], w_in.at[slot, :, pl.ds(QCOLS, HEAD_DIM)]),
            load(wv.at[rows, :], w_in.at[slot, :, pl.ds(QCOLS + HEAD_DIM, HEAD_DIM)]),
        ])
    wo_loads = {}
    for slot in (3, 1, 2, 0):
        columns = pl.ds(pl.multiple_of(src[slot] * FEAT, FEAT), FEAT)
        wo_loads[slot] = load(wo.at[:, columns], w_out.at[slot])

    own_questions = questions[...].astype(F32)
    half_f = FEAT // 2
    qpack[0] = jnp.concatenate(
        [own_questions[:, :half_f], own_questions[:, half_f:]], axis=0
    ).astype(BF16)

    partners = [left, right, opposite]
    partners += [p_peer(d) for d in range(1, n_p)] + [z_peer(d) for d in range(1, NZ)]
    barrier = pltpu.get_barrier_semaphore()
    for partner in partners:
        pl.semaphore_signal(barrier, inc=1, device_id=partner, device_id_type=MESH)
    pl.semaphore_wait(barrier, len(partners))

    copies = []

    def send(source, target, device):
        index = len(copies)
        copy = pltpu.make_async_remote_copy(
            src_ref=source, dst_ref=target, send_sem=send_sem.at[index],
            recv_sem=recv_sem.at[index], device_id=device, device_id_type=MESH,
        )
        copy.start()
        copies.append(copy)
        return copy

    q_in = [
        send(qpack.at[0], qpack.at[1], right),
        send(qpack.at[0], qpack.at[2], left),
        send(qpack.at[0], qpack.at[3], opposite),
    ]
    top, bottom = pl.ds(0, BLK // 2), pl.ds(BLK // 2, BLK // 2)
    r_top = send(tokens.at[top], tok.at[1, top], right)
    l_bottom = send(tokens.at[bottom], tok.at[2, bottom], left)
    r_bottom = send(tokens.at[bottom], tok.at[1, bottom], right)
    l_top = send(tokens.at[top], tok.at[2, top], left)

    tok_load.wait()
    for copy in w_loads[0]:
        copy.wait()
    acc[...] = dot_nn(tok[0], w_in[0])
    row = lax.broadcasted_iota(jnp.int32, (BLK, HEAD_DIM), 0)
    cosine, sine = angles(row + c * BLK)
    q_row = lax.broadcasted_iota(jnp.int32, (QROW, HEAD_DIM), 0)
    q_places = jnp.zeros((QROW, HEAD_DIM), jnp.int32)
    for r in range(QROW):
        q_places = jnp.where(q_row == r, positions[c * QROW + r], q_places)
    q_cosine, q_sine = angles(q_places)

    for slot in range(1, NX):
        for copy in w_loads[slot]:
            copy.wait()
    q_total = jnp.zeros((2 * QROW, QCOLS), F32)
    for slot in (0, 1, 2, 3):
        if slot:
            q_in[slot - 1].wait_recv()
        packed = qpack[slot].astype(F32)
        rows = jnp.concatenate([packed[:QROW], packed[QROW:]], axis=1)
        rows = jnp.concatenate([rows, jnp.zeros_like(rows)], axis=0).astype(BF16)
        q_total = q_total + dot_nn(rows, w_in[slot, :, :QCOLS])
    q_heads = [
        rotate(q_total[:QROW, h * HEAD_DIM:(h + 1) * HEAD_DIM], q_cosine, q_sine)
        for h in range(HEADS)
    ]
    qz[0] = jnp.concatenate(q_heads, axis=0).astype(BF16)
    qz_in = [send(qz.at[0], qz.at[d], z_peer(d)) for d in range(1, NZ)]

    r_top.wait_recv()
    r_pass = send(tok.at[1, top], tok.at[3, top], right)
    l_bottom.wait_recv()
    l_pass = send(tok.at[2, bottom], tok.at[3, bottom], left)
    r_bottom.wait_recv()
    acc[...] += dot_nn(tok[1], w_in[1])
    l_top.wait_recv()
    acc[...] += dot_nn(tok[2], w_in[2])
    r_pass.wait_recv()
    l_pass.wait_recv()
    key_value = acc[:, QCOLS:] + dot_nn(tok[3], w_in[3, :, QCOLS:])
    kvb[0, 0, :BLK] = rotate(key_value[:, :HEAD_DIM], cosine, sine).astype(BF16)
    kvb[0, 0, BLK:] = key_value[:, HEAD_DIM:].astype(BF16)

    a1_in = []
    for d in range(1, n_p):
        there = pl.ds(pl.multiple_of(lax.rem(p + d, n_p) * piece, piece), piece)
        a1_in.append(send(kvb.at[0, 0, there], a1.at[d], p_peer(d)))
    kv_in = [send(kvb.at[0, 0], kvb.at[0, d], y_peer(d)) for d in range(1, NY)]

    for h in range(HEADS):
        columns = slice(h * HEAD_DIM, (h + 1) * HEAD_DIM)
        query = acc[:, columns] + dot_nn(tok[3], w_in[3, :, columns])
        q4[h * BLK:(h + 1) * BLK] = rotate(query, cosine, sine).astype(BF16)
    key_at = lax.broadcasted_iota(jnp.int32, (HEADS * BLK, BLK), 1)
    query_at = lax.rem(lax.broadcasted_iota(jnp.int32, (HEADS * BLK, BLK), 0), BLK)
    seen = (key_at <= query_at) & (key_at < lengths[c])
    scores = jnp.where(seen, dot_nt(q4[...], kvb[0, 0, :BLK]) * SCALE, NEG_BIG)
    own_max = jnp.max(scores, axis=1, keepdims=True)
    weights = jnp.where(seen, jnp.exp(scores - own_max), 0.0)
    own_sum = jnp.sum(weights, axis=1, keepdims=True)
    own_value = dot_nn(weights.astype(BF16), kvb[0, 0, BLK:])

    anchor_block = anchor[0]
    anchor_p = lax.div(anchor_block, NC * NZ) * NC + lax.rem(anchor_block, NC)
    anchor_z = lax.rem(lax.div(anchor_block, NC), NZ)

    def pick(chosen, wanted, index, block):
        here = jnp.zeros((piece, HEAD_DIM), jnp.int32) + wanted
        return jnp.where(here == index, block.astype(F32), chosen)

    mine = pl.ds(pl.multiple_of(p * piece, piece), piece)
    chosen = kvb[0, 0, mine].astype(F32)
    for d in range(1, n_p):
        a1_in[d - 1].wait_recv()
        chosen = pick(chosen, anchor_p, lax.rem(p + n_p - d, n_p), a1[d])
    a2[0] = chosen.astype(BF16)
    a2_in = [send(a2.at[0], a2.at[d], z_peer(d)) for d in range(1, NZ)]

    for copy in kv_in:
        copy.wait_recv()
    sib_in = send(kvb.at[0], kvb.at[1], sibling) if NC > 1 else None

    for d in range(1, NZ):
        a2_in[d - 1].wait_recv()
        chosen = pick(chosen, anchor_z, lax.rem(z + NZ - d, NZ), a2[d])
    anc[mine] = chosen.astype(BF16)
    a3_in = [send(anc.at[mine], anc.at[mine], p_peer(d)) for d in range(1, n_p)]

    n_q = NZ * HEADS * QROW
    lane = lax.broadcasted_iota(jnp.int32, (1, n_q), 1)
    reach = jnp.zeros((1, n_q), jnp.int32)
    for d in range(NZ):
        there = at(y, lax.rem(z + NZ - d, NZ), core) * QROW
        for r in range(QROW):
            spot = (lax.div(lane, HEADS * QROW) == d) & (lax.rem(lane, QROW) == r)
            reach = jnp.where(spot, positions[there + r], reach)
    for copy in qz_in:
        copy.wait_recv()
    queries = qz[...].reshape(n_q, HEAD_DIM)
    if sib_in is not None:
        sib_in.wait_recv()
    blocks = []
    key_row = lax.broadcasted_iota(jnp.int32, (BLK, n_q), 0)
    part_max = jnp.full((1, n_q), NEG_BIG, F32)
    for k in range(NC):
        for d in range(NY):
            number = at(lax.rem(y + NY - d, NY), z, core if k == 0 else 1 - core)
            visible = (key_row < lengths[number]) & (key_row + number * BLK <= reach)
            block_scores = dot_nt(kvb[k, d, :BLK], queries) * SCALE
            block_scores = jnp.where(visible, block_scores, NEG_BIG)
            part_max = jnp.maximum(part_max, jnp.max(block_scores, axis=0, keepdims=True))
            blocks.append((k, d, visible, block_scores))
    part_sum = jnp.zeros((1, n_q), F32)
    part_value = jnp.zeros((n_q, HEAD_DIM), F32)
    for k, d, visible, block_scores in blocks:
        block_weights = jnp.where(visible, jnp.exp(block_scores - part_max), 0.0)
        part_sum = part_sum + jnp.sum(block_weights, axis=0, keepdims=True)
        part_value = part_value + dot_tn(block_weights.astype(BF16), kvb[k, d, BLK:])
    n_r = HEADS * QROW
    part[...] = part_value.astype(BF16).reshape(NZ, n_r, HEAD_DIM)
    stats[0:1] = part_max
    stats[1:2] = part_sum
    stats[2:8] = jnp.zeros((6, n_q), F32)
    lanes = min(n_q, 128)
    part_ins = {}
    for d in range(1, NZ):
        back = z_peer(NZ - d)
        group = pl.ds(d * n_r // lanes * lanes, lanes)
        part_ins[NZ - d] = (
            send(part.at[d], part_in.at[NZ - d], back),
            send(stats.at[:, group], stats_in.at[NZ - d], back),
        )

    for copy in a3_in:
        copy.wait_recv()
    far = (key_at < lengths[anchor_block]) & (jnp.zeros_like(key_at) + anchor_block != c)
    scores = jnp.where(far, dot_nt(q4[...], anc[:BLK]) * SCALE, NEG_BIG)
    row_max = jnp.maximum(own_max, jnp.max(scores, axis=1, keepdims=True))
    weights = jnp.where(far, jnp.exp(scores - row_max), 0.0)
    own_factor = jnp.exp(own_max - row_max)
    total = jnp.sum(weights, axis=1, keepdims=True) + own_sum * own_factor
    value = dot_nn(weights.astype(BF16), anc[BLK:]) + own_value * own_factor
    value = (value / total).astype(BF16)
    attended = jnp.concatenate([value[h * BLK:(h + 1) * BLK] for h in range(HEADS)], axis=1)

    hb = BLK // 2
    wo_loads[3].wait()
    tr_out[...] = dot_nn(attended, w_out[3]).astype(BF16)
    tr_r = send(tr_out.at[top], tr_in.at[top], right)
    tr_l = send(tr_out.at[bottom], tr_in.at[bottom], left)
    wo_loads[2].wait()
    right_term = dot_nn(attended, w_out[2])
    to_right[hb:] = right_term[hb:].astype(BF16)
    pure_r = send(to_right.at[bottom], from_left.at[bottom], right)
    wo_loads[1].wait()
    left_term = dot_nn(attended, w_out[1])
    to_left[:hb] = left_term[:hb].astype(BF16)
    pure_l = send(to_left.at[top], from_right.at[top], left)
    wo_loads[0].wait()
    own_term[...] = dot_nn(attended, w_out[0])
    tr_r.wait_recv()
    to_right[:hb] = (right_term[:hb] + tr_in[:hb].astype(F32)).astype(BF16)
    sum_r = send(to_right.at[top], from_left.at[top], right)
    tr_l.wait_recv()
    to_left[hb:] = (left_term[hb:] + tr_in[hb:].astype(F32)).astype(BF16)
    sum_l = send(to_left.at[bottom], from_right.at[bottom], left)

    eye_row = lax.broadcasted_iota(jnp.int32, (n_r, lanes), 0)
    eye_lane = lax.broadcasted_iota(jnp.int32, (n_r, lanes), 1)

    def column(row_of_stats, slot):
        spot = eye_lane == eye_row + (slot * n_r) % lanes
        return jnp.sum(jnp.where(spot, row_of_stats, 0.0), axis=1, keepdims=True)

    maxima, sums, values = [], [], []
    for d in range(NZ):
        if d == 0:
            held, block = stats[:, 0:lanes], part[0]
        else:
            part_ins[d][0].wait_recv()
            part_ins[d][1].wait_recv()
            held, block = stats_in[d], part_in[d]
        slot = (NZ - d) % NZ
        maxima.append(column(held[0:1], slot))
        sums.append(column(held[1:2], slot))
        values.append(block.astype(F32))
    top_max = maxima[0]
    for one in maxima[1:]:
        top_max = jnp.maximum(top_max, one)
    all_sum = jnp.zeros((n_r, 1), F32)
    all_value = jnp.zeros((n_r, HEAD_DIM), F32)
    for one_max, one_sum, one_value in zip(maxima, sums, values):
        factor = jnp.exp(one_max - top_max)
        all_sum = all_sum + one_sum * factor
        all_value = all_value + one_value * factor
    all_value = all_value / all_sum
    q_att = jnp.concatenate([all_value[h * QROW:(h + 1) * QROW] for h in range(HEADS)], axis=1)
    q_att = jnp.concatenate([q_att, jnp.zeros_like(q_att)], axis=0).astype(BF16)
    qx_in_copies = []
    for slot, device in ((3, opposite), (2, right), (1, left)):
        term = dot_nn(q_att, w_out[slot])[:QROW]
        qx_out[slot] = jnp.concatenate([term[:, :half_f], term[:, half_f:]], axis=0).astype(BF16)
        qx_in_copies.append(send(qx_out.at[slot], qx_in.at[slot], device))
    q_own = dot_nn(q_att, w_out[0])[:QROW]

    for copy in (pure_r, pure_l, sum_r, sum_l):
        copy.wait_recv()
    ctx_out[...] = (
        own_term[...] + from_left[...].astype(F32) + from_right[...].astype(F32)
    ).astype(BF16)
    for copy in qx_in_copies:
        copy.wait_recv()
    for slot in (1, 2, 3):
        packed = qx_in[slot].astype(F32)
        q_own = q_own + jnp.concatenate([packed[:QROW], packed[QROW:]], axis=1)
    q_out[...] = q_own.astype(BF16)
    for copy in copies:
        copy.wait_send()


def local(tokens, questions, q_weight, k_weight, v_weight, o_weight, anchor, lengths, positions):
    n_q = NZ * HEADS * QROW
    n_r = HEADS * QROW
    lanes = min(n_q, 128)
    piece = 2 * BLK // (NY * NC)
    anywhere = pl.BlockSpec(memory_space=pl.ANY)
    vmem = pl.BlockSpec(memory_space=pltpu.VMEM)
    smem = pl.BlockSpec(memory_space=pltpu.SMEM)
    return pl.pallas_call(
        kernel,
        out_shape=(
            jax.ShapeDtypeStruct((BLK, FEAT), BF16),
            jax.ShapeDtypeStruct((QROW, FEAT), BF16),
        ),
        in_specs=[anywhere, vmem] + [anywhere] * 4 + [smem] * 3,
        out_specs=(vmem, vmem),
        scratch_shapes=[
            pltpu.VMEM((NX, FEAT, WCOLS), BF16),
            pltpu.VMEM((NX, QCOLS, FEAT), BF16),
            pltpu.VMEM((NX, BLK, FEAT), BF16),
            pltpu.VMEM((NX, 2 * QROW, FEAT // 2), BF16),
            pltpu.VMEM((BLK, WCOLS), F32),
            pltpu.VMEM((HEADS * BLK, HEAD_DIM), BF16),
            pltpu.VMEM((NZ, n_r, HEAD_DIM), BF16),
            pltpu.VMEM((NC, NY, 2 * BLK, HEAD_DIM), BF16),
            pltpu.VMEM((NY * NC, piece, HEAD_DIM), BF16),
            pltpu.VMEM((NZ, piece, HEAD_DIM), BF16),
            pltpu.VMEM((2 * BLK, HEAD_DIM), BF16),
            pltpu.VMEM((NZ, n_r, HEAD_DIM), BF16),
            pltpu.VMEM((8, n_q), F32),
            pltpu.VMEM((NZ, n_r, HEAD_DIM), BF16),
            pltpu.VMEM((NZ, 8, lanes), F32),
            pltpu.VMEM((BLK, FEAT), BF16),
            pltpu.VMEM((BLK, FEAT), BF16),
            pltpu.VMEM((BLK, FEAT), BF16),
            pltpu.VMEM((BLK, FEAT), BF16),
            pltpu.VMEM((BLK, FEAT), BF16),
            pltpu.VMEM((BLK, FEAT), BF16),
            pltpu.VMEM((BLK, FEAT), F32),
            pltpu.VMEM((NX, 2 * QROW, FEAT // 2), BF16),
            pltpu.VMEM((NX, 2 * QROW, FEAT // 2), BF16),
            pltpu.SemaphoreType.DMA((N_LOADS,)),
            pltpu.SemaphoreType.DMA((N_COPIES,)),
            pltpu.SemaphoreType.DMA((N_COPIES,)),
        ],
        compiler_params=pltpu.CompilerParams(
            collective_id=0, has_side_effects=True, vmem_limit_bytes=48 * 2**20
        ),
        name="fused_attention",
    )(tokens, questions, q_weight, k_weight, v_weight, o_weight, anchor, lengths, positions)


def solution(mesh):
    in_specs = (
        P("ctx", "kvg"),
        P("ctx", "kvg"),
        P(None, "kvg"),
        P(None, "kvg"),
        P(None, "kvg"),
        P("kvg", None),
        P(),
        P(),
        P(),
    )
    out_specs = (P("ctx", "kvg"), P("ctx", "kvg"))
    return jax.shard_map(local, mesh=mesh, in_specs=in_specs, out_specs=out_specs, check_vma=False)
```

```python
import math

import jax
import jax.numpy as jnp
from jax import lax
from jax.experimental import pallas as pl
from jax.experimental.pallas import tpu as pltpu
from jax.sharding import PartitionSpec as P

HEAD_DIM = 128
NX = 4
NY, NZ, NC = 4, 8, 2
BLK = 128
QROW = 8
HEADS = 4
FEAT = 1024
QCOLS = HEADS * HEAD_DIM
WCOLS = QCOLS + 2 * HEAD_DIM
NEG_BIG = -1e30
SCALE = HEAD_DIM ** (-0.5)
F32 = jnp.float32
BF16 = jnp.bfloat16
MESH = pl.DeviceIdType.MESH
N_COPIES = 80
N_LOADS = 20


def dot_nn(a, b):
    return jnp.dot(a, b, preferred_element_type=F32)


def dot_nt(a, b):
    return lax.dot_general(a, b, (((1,), (1,)), ((), ())), preferred_element_type=F32)


def dot_tn(a, b):
    return lax.dot_general(a, b, (((0,), (0,)), ((), ())), preferred_element_type=F32)


def angles(places):
    lane = lax.broadcasted_iota(jnp.int32, places.shape, 1)
    half = HEAD_DIM // 2
    index = jnp.where(lane < half, lane, lane - half).astype(F32)
    frequency = jnp.exp(index * (-2.0 * math.log(500000.0) / HEAD_DIM))
    angle = places.astype(F32) * frequency
    sine = jnp.sin(angle)
    return jnp.cos(angle), jnp.where(lane < half, -sine, sine)


def rotate(head, cosine, sine):
    return head * cosine + pltpu.roll(head, HEAD_DIM // 2, 1) * sine


def kernel(
    tokens, questions, wq, wk, wv, wo, anchor, lengths, positions,
    ctx_out, q_out,
    asked, lengths_s, positions_s, w_in, w_out, tok, qpack, acc, q4, qz, kvb, a1, a2, anc,
    part, stats, part_in, stats_in, tr_out, tr_in, to_right, to_left, from_left, from_right,
    own_term, qx_out, qx_in, load_sem, send_sem, recv_sem,
):
    n_p = NY * NC
    piece = 2 * BLK // n_p
    c = lax.axis_index("ctx")
    g = lax.axis_index("kvg")
    core = lax.rem(c, NC)
    z = lax.rem(lax.div(c, NC), NZ)
    y = lax.div(c, NC * NZ)
    p = y * NC + core

    def at(y_, z_, core_):
        return (y_ * NZ + z_) * NC + core_

    src = [g, lax.rem(g + 3, NX), lax.rem(g + 1, NX), lax.rem(g + 2, NX)]
    left, right, opposite = (c, src[1]), (c, src[2]), (c, src[3])

    def p_peer(d):
        q = lax.rem(p + d, n_p)
        return (at(lax.div(q, NC), z, lax.rem(q, NC)), g)

    def z_peer(d):
        return (at(y, lax.rem(z + d, NZ), core), g)

    def y_peer(d):
        return (at(lax.rem(y + d, NY), z, core), g)

    sibling = (at(y, z, 1 - core), g)

    loads = []

    def load(source, target):
        copy = pltpu.make_async_copy(source, target, load_sem.at[len(loads)])
        copy.start()
        loads.append(copy)
        return copy

    asked_load = load(questions, asked)
    scalar_loads = [load(lengths, lengths_s), load(positions, positions_s)]
    tok_load = load(tokens, tok.at[0])
    w_loads = []
    for slot in range(NX):
        rows = pl.ds(pl.multiple_of(src[slot] * FEAT, FEAT), FEAT)
        w_loads.append([
            load(wq.at[rows, :], w_in.at[slot, :, pl.ds(0, QCOLS)]),
            load(wk.at[rows, :], w_in.at[slot, :, pl.ds(QCOLS, HEAD_DIM)]),
            load(wv.at[rows, :], w_in.at[slot, :, pl.ds(QCOLS + HEAD_DIM, HEAD_DIM)]),
        ])
    wo_loads = {}
    for slot in (3, 1, 2, 0):
        columns = pl.ds(pl.multiple_of(src[slot] * FEAT, FEAT), FEAT)
        wo_loads[slot] = load(wo.at[:, columns], w_out.at[slot])

    asked_load.wait()
    own_questions = asked[...].astype(F32)
    half_f = FEAT // 2
    qpack[0] = jnp.concatenate(
        [own_questions[:, :half_f], own_questions[:, half_f:]], axis=0
    ).astype(BF16)

    partners = [left, right, opposite]
    partners += [p_peer(d) for d in range(1, n_p)] + [z_peer(d) for d in range(1, NZ)]
    barrier = pltpu.get_barrier_semaphore()
    for partner in partners:
        pl.semaphore_signal(barrier, inc=1, device_id=partner, device_id_type=MESH)
    pl.semaphore_wait(barrier, len(partners))

    copies = []

    def send(source, target, device):
        index = len(copies)
        copy = pltpu.make_async_remote_copy(
            src_ref=source, dst_ref=target, send_sem=send_sem.at[index],
            recv_sem=recv_sem.at[index], device_id=device, device_id_type=MESH,
        )
        copy.start()
        copies.append(copy)
        return copy

    q_in = [
        send(qpack.at[0], qpack.at[1], right),
        send(qpack.at[0], qpack.at[2], left),
        send(qpack.at[0], qpack.at[3], opposite),
    ]
    top, bottom = pl.ds(0, BLK // 2), pl.ds(BLK // 2, BLK // 2)
    r_top = send(tokens.at[top], tok.at[1, top], right)
    l_bottom = send(tokens.at[bottom], tok.at[2, bottom], left)
    r_bottom = send(tokens.at[bottom], tok.at[1, bottom], right)
    l_top = send(tokens.at[top], tok.at[2, top], left)

    tok_load.wait()
    for copy in w_loads[0]:
        copy.wait()
    acc[...] = dot_nn(tok[0], w_in[0])
    row = lax.broadcasted_iota(jnp.int32, (BLK, HEAD_DIM), 0)
    cosine, sine = angles(row + c * BLK)
    for copy in scalar_loads:
        copy.wait()
    q_row = lax.broadcasted_iota(jnp.int32, (QROW, HEAD_DIM), 0)
    q_places = jnp.zeros((QROW, HEAD_DIM), jnp.int32)
    for r in range(QROW):
        q_places = jnp.where(q_row == r, positions_s[c * QROW + r], q_places)
    q_cosine, q_sine = angles(q_places)

    for slot in range(1, NX):
        for copy in w_loads[slot]:
            copy.wait()
    q_total = jnp.zeros((2 * QROW, QCOLS), F32)
    for slot in (0, 1, 2, 3):
        if slot:
            q_in[slot - 1].wait_recv()
        packed = qpack[slot].astype(F32)
        rows = jnp.concatenate([packed[:QROW], packed[QROW:]], axis=1)
        rows = jnp.concatenate([rows, jnp.zeros_like(rows)], axis=0).astype(BF16)
        q_total = q_total + dot_nn(rows, w_in[slot, :, :QCOLS])
    q_heads = [
        rotate(q_total[:QROW, h * HEAD_DIM:(h + 1) * HEAD_DIM], q_cosine, q_sine)
        for h in range(HEADS)
    ]
    qz[0] = jnp.concatenate(q_heads, axis=0).astype(BF16)
    qz_in = [send(qz.at[0], qz.at[d], z_peer(d)) for d in range(1, NZ)]

    r_top.wait_recv()
    r_pass = send(tok.at[1, top], tok.at[3, top], right)
    l_bottom.wait_recv()
    l_pass = send(tok.at[2, bottom], tok.at[3, bottom], left)
    r_bottom.wait_recv()
    acc[...] += dot_nn(tok[1], w_in[1])
    l_top.wait_recv()
    acc[...] += dot_nn(tok[2], w_in[2])
    r_pass.wait_recv()
    l_pass.wait_recv()
    key_value = acc[:, QCOLS:] + dot_nn(tok[3], w_in[3, :, QCOLS:])
    kvb[0, 0, :BLK] = rotate(key_value[:, :HEAD_DIM], cosine, sine).astype(BF16)
    kvb[0, 0, BLK:] = key_value[:, HEAD_DIM:].astype(BF16)

    a1_in = []
    for d in range(1, n_p):
        there = pl.ds(pl.multiple_of(lax.rem(p + d, n_p) * piece, piece), piece)
        a1_in.append(send(kvb.at[0, 0, there], a1.at[d], p_peer(d)))
    kv_in = [send(kvb.at[0, 0], kvb.at[0, d], y_peer(d)) for d in range(1, NY)]

    for h in range(HEADS):
        columns = slice(h * HEAD_DIM, (h + 1) * HEAD_DIM)
        query = acc[:, columns] + dot_nn(tok[3], w_in[3, :, columns])
        q4[h * BLK:(h + 1) * BLK] = rotate(query, cosine, sine).astype(BF16)
    key_at = lax.broadcasted_iota(jnp.int32, (HEADS * BLK, BLK), 1)
    query_at = lax.rem(lax.broadcasted_iota(jnp.int32, (HEADS * BLK, BLK), 0), BLK)
    seen = (key_at <= query_at) & (key_at < lengths_s[c])
    scores = jnp.where(seen, dot_nt(q4[...], kvb[0, 0, :BLK]) * SCALE, NEG_BIG)
    own_max = jnp.max(scores, axis=1, keepdims=True)
    weights = jnp.where(seen, jnp.exp(scores - own_max), 0.0)
    own_sum = jnp.sum(weights, axis=1, keepdims=True)
    own_value = dot_nn(weights.astype(BF16), kvb[0, 0, BLK:])

    anchor_block = anchor[0]
    anchor_p = lax.div(anchor_block, NC * NZ) * NC + lax.rem(anchor_block, NC)
    anchor_z = lax.rem(lax.div(anchor_block, NC), NZ)

    def pick(chosen, wanted, index, block):
        here = jnp.zeros((piece, HEAD_DIM), jnp.int32) + wanted
        return jnp.where(here == index, block.astype(F32), chosen)

    mine = pl.ds(pl.multiple_of(p * piece, piece), piece)
    chosen = kvb[0, 0, mine].astype(F32)
    for d in range(1, n_p):
        a1_in[d - 1].wait_recv()
        chosen = pick(chosen, anchor_p, lax.rem(p + n_p - d, n_p), a1[d])
    a2[0] = chosen.astype(BF16)
    a2_in = [send(a2.at[0], a2.at[d], z_peer(d)) for d in range(1, NZ)]

    for copy in kv_in:
        copy.wait_recv()
    sib_in = send(kvb.at[0], kvb.at[1], sibling) if NC > 1 else None

    for d in range(1, NZ):
        a2_in[d - 1].wait_recv()
        chosen = pick(chosen, anchor_z, lax.rem(z + NZ - d, NZ), a2[d])
    anc[mine] = chosen.astype(BF16)
    a3_in = [send(anc.at[mine], anc.at[mine], p_peer(d)) for d in range(1, n_p)]

    n_q = NZ * HEADS * QROW
    lane = lax.broadcasted_iota(jnp.int32, (1, n_q), 1)
    reach = jnp.zeros((1, n_q), jnp.int32)
    for d in range(NZ):
        there = at(y, lax.rem(z + NZ - d, NZ), core) * QROW
        for r in range(QROW):
            spot = (lax.div(lane, HEADS * QROW) == d) & (lax.rem(lane, QROW) == r)
            reach = jnp.where(spot, positions_s[there + r], reach)
    for copy in qz_in:
        copy.wait_recv()
    queries = qz[...].reshape(n_q, HEAD_DIM)
    if sib_in is not None:
        sib_in.wait_recv()
    blocks = []
    key_row = lax.broadcasted_iota(jnp.int32, (BLK, n_q), 0)
    part_max = jnp.full((1, n_q), NEG_BIG, F32)
    for k in range(NC):
        for d in range(NY):
            number = at(lax.rem(y + NY - d, NY), z, core if k == 0 else 1 - core)
            visible = (key_row < lengths_s[number]) & (key_row + number * BLK <= reach)
            block_scores = dot_nt(kvb[k, d, :BLK], queries) * SCALE
            block_scores = jnp.where(visible, block_scores, NEG_BIG)
            part_max = jnp.maximum(part_max, jnp.max(block_scores, axis=0, keepdims=True))
            blocks.append((k, d, visible, block_scores))
    part_sum = jnp.zeros((1, n_q), F32)
    part_value = jnp.zeros((n_q, HEAD_DIM), F32)
    for k, d, visible, block_scores in blocks:
        block_weights = jnp.where(visible, jnp.exp(block_scores - part_max), 0.0)
        part_sum = part_sum + jnp.sum(block_weights, axis=0, keepdims=True)
        part_value = part_value + dot_tn(block_weights.astype(BF16), kvb[k, d, BLK:])
    n_r = HEADS * QROW
    part[...] = part_value.astype(BF16).reshape(NZ, n_r, HEAD_DIM)
    stats[0:1] = part_max
    stats[1:2] = part_sum
    stats[2:8] = jnp.zeros((6, n_q), F32)
    lanes = min(n_q, 128)
    part_ins = {}
    for d in range(1, NZ):
        back = z_peer(NZ - d)
        group = pl.ds(d * n_r // lanes * lanes, lanes)
        part_ins[NZ - d] = (
            send(part.at[d], part_in.at[NZ - d], back),
            send(stats.at[:, group], stats_in.at[NZ - d], back),
        )

    for copy in a3_in:
        copy.wait_recv()
    far = (key_at < lengths_s[anchor_block]) & (jnp.zeros_like(key_at) + anchor_block != c)
    scores = jnp.where(far, dot_nt(q4[...], anc[:BLK]) * SCALE, NEG_BIG)
    row_max = jnp.maximum(own_max, jnp.max(scores, axis=1, keepdims=True))
    weights = jnp.where(far, jnp.exp(scores - row_max), 0.0)
    own_factor = jnp.exp(own_max - row_max)
    total = jnp.sum(weights, axis=1, keepdims=True) + own_sum * own_factor
    value = dot_nn(weights.astype(BF16), anc[BLK:]) + own_value * own_factor
    value = (value / total).astype(BF16)
    attended = jnp.concatenate([value[h * BLK:(h + 1) * BLK] for h in range(HEADS)], axis=1)

    hb = BLK // 2
    wo_loads[3].wait()
    tr_out[...] = dot_nn(attended, w_out[3]).astype(BF16)
    tr_r = send(tr_out.at[top], tr_in.at[top], right)
    tr_l = send(tr_out.at[bottom], tr_in.at[bottom], left)
    wo_loads[2].wait()
    right_term = dot_nn(attended, w_out[2])
    to_right[hb:] = right_term[hb:].astype(BF16)
    pure_r = send(to_right.at[bottom], from_left.at[bottom], right)
    wo_loads[1].wait()
    left_term = dot_nn(attended, w_out[1])
    to_left[:hb] = left_term[:hb].astype(BF16)
    pure_l = send(to_left.at[top], from_right.at[top], left)
    wo_loads[0].wait()
    own_term[...] = dot_nn(attended, w_out[0])
    tr_r.wait_recv()
    to_right[:hb] = (right_term[:hb] + tr_in[:hb].astype(F32)).astype(BF16)
    sum_r = send(to_right.at[top], from_left.at[top], right)
    tr_l.wait_recv()
    to_left[hb:] = (left_term[hb:] + tr_in[hb:].astype(F32)).astype(BF16)
    sum_l = send(to_left.at[bottom], from_right.at[bottom], left)

    eye_row = lax.broadcasted_iota(jnp.int32, (n_r, lanes), 0)
    eye_lane = lax.broadcasted_iota(jnp.int32, (n_r, lanes), 1)

    def column(row_of_stats, slot):
        spot = eye_lane == eye_row + (slot * n_r) % lanes
        return jnp.sum(jnp.where(spot, row_of_stats, 0.0), axis=1, keepdims=True)

    maxima, sums, values = [], [], []
    for d in range(NZ):
        if d == 0:
            held, block = stats[:, 0:lanes], part[0]
        else:
            part_ins[d][0].wait_recv()
            part_ins[d][1].wait_recv()
            held, block = stats_in[d], part_in[d]
        slot = (NZ - d) % NZ
        maxima.append(column(held[0:1], slot))
        sums.append(column(held[1:2], slot))
        values.append(block.astype(F32))
    top_max = maxima[0]
    for one in maxima[1:]:
        top_max = jnp.maximum(top_max, one)
    all_sum = jnp.zeros((n_r, 1), F32)
    all_value = jnp.zeros((n_r, HEAD_DIM), F32)
    for one_max, one_sum, one_value in zip(maxima, sums, values):
        factor = jnp.exp(one_max - top_max)
        all_sum = all_sum + one_sum * factor
        all_value = all_value + one_value * factor
    all_value = all_value / all_sum
    q_att = jnp.concatenate([all_value[h * QROW:(h + 1) * QROW] for h in range(HEADS)], axis=1)
    q_att = jnp.concatenate([q_att, jnp.zeros_like(q_att)], axis=0).astype(BF16)
    qx_in_copies = []
    for slot, device in ((3, opposite), (2, right), (1, left)):
        term = dot_nn(q_att, w_out[slot])[:QROW]
        qx_out[slot] = jnp.concatenate([term[:, :half_f], term[:, half_f:]], axis=0).astype(BF16)
        qx_in_copies.append(send(qx_out.at[slot], qx_in.at[slot], device))
    q_own = dot_nn(q_att, w_out[0])[:QROW]

    for copy in (pure_r, pure_l, sum_r, sum_l):
        copy.wait_recv()
    ctx_out[...] = (
        own_term[...] + from_left[...].astype(F32) + from_right[...].astype(F32)
    ).astype(BF16)
    for copy in qx_in_copies:
        copy.wait_recv()
    for slot in (1, 2, 3):
        packed = qx_in[slot].astype(F32)
        q_own = q_own + jnp.concatenate([packed[:QROW], packed[QROW:]], axis=1)
    q_out[...] = q_own.astype(BF16)
    for copy in copies:
        copy.wait_send()


def local(tokens, questions, q_weight, k_weight, v_weight, o_weight, anchor, lengths, positions):
    n_q = NZ * HEADS * QROW
    n_r = HEADS * QROW
    lanes = min(n_q, 128)
    piece = 2 * BLK // (NY * NC)
    anywhere = pl.BlockSpec(memory_space=pltpu.HBM)
    vmem = pl.BlockSpec(memory_space=pltpu.VMEM)
    smem = pl.BlockSpec(memory_space=pltpu.SMEM)
    operands = [
        pltpu.with_memory_space_constraint(x, pltpu.HBM)
        for x in (tokens, questions, q_weight, k_weight, v_weight, o_weight)
    ]
    lengths, positions = [
        pltpu.with_memory_space_constraint(x, pltpu.HBM) for x in (lengths, positions)
    ]
    return pl.pallas_call(
        kernel,
        out_shape=(
            jax.ShapeDtypeStruct((BLK, FEAT), BF16),
            jax.ShapeDtypeStruct((QROW, FEAT), BF16),
        ),
        in_specs=[anywhere] * 6 + [smem] + [anywhere] * 2,
        out_specs=(vmem, vmem),
        scratch_shapes=[
            pltpu.VMEM((QROW, FEAT), BF16),
            pltpu.SMEM(lengths.shape, jnp.int32),
            pltpu.SMEM(positions.shape, jnp.int32),
            pltpu.VMEM((NX, FEAT, WCOLS), BF16),
            pltpu.VMEM((NX, QCOLS, FEAT), BF16),
            pltpu.VMEM((NX, BLK, FEAT), BF16),
            pltpu.VMEM((NX, 2 * QROW, FEAT // 2), BF16),
            pltpu.VMEM((BLK, WCOLS), F32),
            pltpu.VMEM((HEADS * BLK, HEAD_DIM), BF16),
            pltpu.VMEM((NZ, n_r, HEAD_DIM), BF16),
            pltpu.VMEM((NC, NY, 2 * BLK, HEAD_DIM), BF16),
            pltpu.VMEM((NY * NC, piece, HEAD_DIM), BF16),
            pltpu.VMEM((NZ, piece, HEAD_DIM), BF16),
            pltpu.VMEM((2 * BLK, HEAD_DIM), BF16),
            pltpu.VMEM((NZ, n_r, HEAD_DIM), BF16),
            pltpu.VMEM((8, n_q), F32),
            pltpu.VMEM((NZ, n_r, HEAD_DIM), BF16),
            pltpu.VMEM((NZ, 8, lanes), F32),
            pltpu.VMEM((BLK, FEAT), BF16),
            pltpu.VMEM((BLK, FEAT), BF16),
            pltpu.VMEM((BLK, FEAT), BF16),
            pltpu.VMEM((BLK, FEAT), BF16),
            pltpu.VMEM((BLK, FEAT), BF16),
            pltpu.VMEM((BLK, FEAT), BF16),
            pltpu.VMEM((BLK, FEAT), F32),
            pltpu.VMEM((NX, 2 * QROW, FEAT // 2), BF16),
            pltpu.VMEM((NX, 2 * QROW, FEAT // 2), BF16),
            pltpu.SemaphoreType.DMA((N_LOADS,)),
            pltpu.SemaphoreType.DMA((N_COPIES,)),
            pltpu.SemaphoreType.DMA((N_COPIES,)),
        ],
        compiler_params=pltpu.CompilerParams(
            collective_id=0, has_side_effects=True, vmem_limit_bytes=40 * 2**20
        ),
        name="fused_attention",
    )(*operands, anchor, lengths, positions)


def solution(mesh):
    in_specs = (
        P("ctx", "kvg"),
        P("ctx", "kvg"),
        P(None, "kvg"),
        P(None, "kvg"),
        P(None, "kvg"),
        P("kvg", None),
        P(),
        P(),
        P(),
    )
    out_specs = (P("ctx", "kvg"), P("ctx", "kvg"))
    return jax.shard_map(local, mesh=mesh, in_specs=in_specs, out_specs=out_specs, check_vma=False)
```

```python
import math

import jax
import jax.numpy as jnp
from jax import lax
from jax.experimental import pallas as pl
from jax.experimental.pallas import tpu as pltpu
from jax.sharding import PartitionSpec as P

HEAD_DIM = 128
NX = 4
NY, NZ, NC = 4, 8, 2
BLK = 128
QROW = 8
HEADS = 4
FEAT = 1024
QCOLS = HEADS * HEAD_DIM
WCOLS = QCOLS + 2 * HEAD_DIM
NEG_BIG = -1e30
SCALE = HEAD_DIM ** (-0.5)
F32 = jnp.float32
BF16 = jnp.bfloat16
MESH = pl.DeviceIdType.MESH
LANES = 128
N_COPIES = 96
N_LOADS = 20


def dot_nn(a, b):
    return jnp.dot(a, b, preferred_element_type=F32)


def dot_nt(a, b):
    return lax.dot_general(a, b, (((1,), (1,)), ((), ())), preferred_element_type=F32)


def dot_tn(a, b):
    return lax.dot_general(a, b, (((0,), (0,)), ((), ())), preferred_element_type=F32)


def angles(places):
    lane = lax.broadcasted_iota(jnp.int32, places.shape, 1)
    half = HEAD_DIM // 2
    index = jnp.where(lane < half, lane, lane - half).astype(F32)
    frequency = jnp.exp(index * (-2.0 * math.log(500000.0) / HEAD_DIM))
    angle = places.astype(F32) * frequency
    sine = jnp.sin(angle)
    return jnp.cos(angle), jnp.where(lane < half, -sine, sine)


def rotate(head, cosine, sine):
    return head * cosine + pltpu.roll(head, HEAD_DIM // 2, 1) * sine


def kernel(
    tokens, questions, wq, wk, wv, wo, anchor, lengths, positions,
    ctx_out, q_out,
    asked, lengths_s, positions_s, w_in, w_out, own_tok, tok, qpack, acc, q4, qz, kvb,
    a_rows, a_tok, a2, anc, part, part_in, tr_out, tr_in, to_right, to_left,
    from_left, from_right, own_term, qx_out, qx_in, load_sem, send_sem, recv_sem,
):
    n_p = NY * NC
    a_len = BLK // n_p
    c = lax.axis_index("ctx")
    g = lax.axis_index("kvg")
    core = lax.rem(c, NC)
    z = lax.rem(lax.div(c, NC), NZ)
    y = lax.div(c, NC * NZ)
    p = y * NC + core

    def at(y_, z_, core_):
        return (y_ * NZ + z_) * NC + core_

    src = [g, lax.rem(g + 3, NX), lax.rem(g + 1, NX), lax.rem(g + 2, NX)]
    left, right, opposite = (c, src[1]), (c, src[2]), (c, src[3])

    def flip(dc):
        return 1 - core if dc else core

    p_steps = [(dy, dc) for dy in range(NY) for dc in range(NC) if dy or dc]
    p_steps.sort(key=lambda s: (-min(s[0], NY - s[0]), -s[1]))
    z_steps = sorted(range(1, NZ), key=lambda d: -min(d, NZ - d))

    def p_peer(dy, dc):
        return (at(lax.rem(y + dy, NY), z, flip(dc)), g)

    def p_index(dy, dc):
        return lax.rem(y + dy, NY) * NC + flip(dc)

    def z_peer(d):
        return (at(y, lax.rem(z + d, NZ), core), g)

    loads = []

    def load(source, target):
        copy = pltpu.make_async_copy(source, target, load_sem.at[len(loads)])
        copy.start()
        loads.append(copy)
        return copy

    asked_load = load(questions, asked)
    scalar_loads = [load(lengths, lengths_s), load(positions, positions_s)]
    tok_load = load(tokens, own_tok)
    w_loads = []
    for slot in range(NX):
        rows = pl.ds(pl.multiple_of(src[slot] * FEAT, FEAT), FEAT)
        w_loads.append([
            load(wq.at[rows, :], w_in.at[slot, :, pl.ds(0, QCOLS)]),
            load(wk.at[rows, :], w_in.at[slot, :, pl.ds(QCOLS, HEAD_DIM)]),
            load(wv.at[rows, :], w_in.at[slot, :, pl.ds(QCOLS + HEAD_DIM, HEAD_DIM)]),
        ])

    partners = [z_peer(d) for d in z_steps] + [opposite]
    partners += [p_peer(dy, dc) for dy, dc in p_steps] + [left, right]
    barrier = pltpu.get_barrier_semaphore()
    for partner in partners:
        pl.semaphore_signal(barrier, inc=1, device_id=partner, device_id_type=MESH)

    asked_load.wait()
    own_questions = asked[...].astype(F32)
    half_f = FEAT // 2
    qpack[0] = jnp.concatenate(
        [own_questions[:, :half_f], own_questions[:, half_f:]], axis=0
    ).astype(BF16)
    pl.semaphore_wait(barrier, len(partners))

    copies = []

    def send(source, target, device):
        index = len(copies)
        copy = pltpu.make_async_remote_copy(
            src_ref=source, dst_ref=target, send_sem=send_sem.at[index],
            recv_sem=recv_sem.at[index], device_id=device, device_id_type=MESH,
        )
        copy.start()
        copies.append(copy)
        return copy

    quarter = FEAT // 4
    near_r, near_l = {}, {}

    def send_tokens(j_r, j_l):
        near_r[j_r] = send(tokens.at[:, pl.ds(j_r * quarter, quarter)], tok.at[1, j_r], right)
        near_l[j_l] = send(tokens.at[:, pl.ds(j_l * quarter, quarter)], tok.at[2, j_l], left)

    send_tokens(0, 3)
    a_in = {}
    for dy, dc in p_steps:
        there = pl.ds(pl.multiple_of(p_index(dy, dc) * a_len, a_len), a_len)
        a_in[dy, dc] = send(tokens.at[there, :], a_rows.at[dy * NC + dc], p_peer(dy, dc))
    send_tokens(1, 2)
    send_tokens(2, 1)
    send_tokens(3, 0)
    q_in = [
        send(qpack.at[0], qpack.at[3], opposite),
        send(qpack.at[0], qpack.at[1], right),
        send(qpack.at[0], qpack.at[2], left),
    ]

    tok_load.wait()
    for copy in w_loads[0]:
        copy.wait()
    acc[...] = dot_nn(own_tok[...], w_in[0])
    row = lax.broadcasted_iota(jnp.int32, (BLK, HEAD_DIM), 0)
    cosine, sine = angles(row + c * BLK)
    for copy in scalar_loads:
        copy.wait()
    q_row = lax.broadcasted_iota(jnp.int32, (QROW, HEAD_DIM), 0)
    q_places = jnp.zeros((QROW, HEAD_DIM), jnp.int32)
    for r in range(QROW):
        q_places = jnp.where(q_row == r, positions_s[c * QROW + r], q_places)
    q_cosine, q_sine = angles(q_places)
    anchor_block = anchor[0]
    anchor_y = lax.div(anchor_block, NC * NZ)
    anchor_core = lax.rem(anchor_block, NC)
    anchor_z = lax.rem(lax.div(anchor_block, NC), NZ)
    a_row = lax.broadcasted_iota(jnp.int32, (a_len, HEAD_DIM), 0)
    a_cosine, a_sine = angles(a_row + p * a_len + anchor_block * BLK)

    far_r, far_l = {}, {}

    def pass_on(j_r, j_l):
        near_r[j_r].wait_recv()
        far_r[j_r] = send(tok.at[1, j_r], tok.at[3, j_r], right)
        near_l[j_l].wait_recv()
        far_l[j_l] = send(tok.at[2, j_l], tok.at[3, j_l], left)

    pass_on(0, 3)
    pass_on(1, 2)

    wanted = jnp.zeros((a_len, FEAT), jnp.int32)
    wanted_p = wanted + (anchor_y * NC + anchor_core)
    chosen = own_tok[pl.ds(pl.multiple_of(p * a_len, a_len), a_len), :].astype(F32)
    for dy, dc in p_steps:
        a_in[dy, dc].wait_recv()
        origin = lax.rem(y + NY - dy, NY) * NC + flip(dc)
        chosen = jnp.where(wanted_p == origin, a_rows[dy * NC + dc].astype(F32), chosen)
    a_tok[0] = chosen.astype(BF16)
    at_in = [
        send(a_tok.at[0], a_tok.at[3], opposite),
        send(a_tok.at[0], a_tok.at[1], right),
        send(a_tok.at[0], a_tok.at[2], left),
    ]

    for slot in (1, 2):
        for copy in w_loads[slot]:
            copy.wait()
    for j in range(2):
        acc[...] += dot_nn(tok[1, j], w_in[1, j * quarter:(j + 1) * quarter])
        k = 3 - j
        acc[...] += dot_nn(tok[2, k], w_in[2, k * quarter:(k + 1) * quarter])
    for j in range(2, 4):
        near_r[j].wait_recv()
        acc[...] += dot_nn(tok[1, j], w_in[1, j * quarter:(j + 1) * quarter])
        k = 3 - j
        near_l[k].wait_recv()
        acc[...] += dot_nn(tok[2, k], w_in[2, k * quarter:(k + 1) * quarter])

    for copy in w_loads[3]:
        copy.wait()
    for copy in q_in:
        copy.wait_recv()
    q_total = jnp.zeros((2 * QROW, QCOLS), F32)
    for slot in range(NX):
        packed = qpack[slot].astype(F32)
        rows = jnp.concatenate([packed[:QROW], packed[QROW:]], axis=1)
        rows = jnp.concatenate([rows, jnp.zeros_like(rows)], axis=0).astype(BF16)
        q_total = q_total + dot_nn(rows, w_in[slot, :, :QCOLS])
    q_heads = [
        rotate(q_total[:QROW, h * HEAD_DIM:(h + 1) * HEAD_DIM], q_cosine, q_sine)
        for h in range(HEADS)
    ]
    qz[0] = jnp.concatenate(q_heads, axis=0).astype(BF16)
    qz_in = [send(qz.at[0], qz.at[d], z_peer(d)) for d in z_steps]

    key_value = acc[:, QCOLS:]
    for j in (0, 3, 1, 2):
        (far_r if j < 2 else far_l)[j].wait_recv()
        key_value = key_value + dot_nn(tok[3, j], w_in[3, j * quarter:(j + 1) * quarter, QCOLS:])
    kvb[0, 0, :BLK] = rotate(key_value[:, :HEAD_DIM], cosine, sine).astype(BF16)
    kvb[0, 0, BLK:] = key_value[:, HEAD_DIM:].astype(BF16)

    for copy in at_in:
        copy.wait_recv()
    a_kv = jnp.zeros((a_len, 2 * HEAD_DIM), F32)
    for slot in range(NX):
        a_kv = a_kv + dot_nn(a_tok[slot], w_in[slot, :, QCOLS:])
    a2[0, :a_len] = rotate(a_kv[:, :HEAD_DIM], a_cosine, a_sine).astype(BF16)
    a2[0, a_len:] = a_kv[:, HEAD_DIM:].astype(BF16)
    a2_in = {d: send(a2.at[0], a2.at[d], z_peer(d)) for d in z_steps}
    kv_in = [
        send(kvb.at[0, 0], kvb.at[0, d], p_peer(d, 0))
        for d in sorted(range(1, NY), key=lambda d: -min(d, NY - d))
    ]
    wo_loads = {}
    for slot in (3, 2, 1, 0):
        columns = pl.ds(pl.multiple_of(src[slot] * FEAT, FEAT), FEAT)
        wo_loads[slot] = load(wo.at[:, columns], w_out.at[slot])

    for h in range(HEADS):
        columns = slice(h * HEAD_DIM, (h + 1) * HEAD_DIM)
        query = acc[:, columns]
        for j in range(4):
            query = query + dot_nn(tok[3, j], w_in[3, j * quarter:(j + 1) * quarter, columns])
        q4[h * BLK:(h + 1) * BLK] = rotate(query, cosine, sine).astype(BF16)
    key_at = lax.broadcasted_iota(jnp.int32, (HEADS * BLK, BLK), 1)
    query_at = lax.rem(lax.broadcasted_iota(jnp.int32, (HEADS * BLK, BLK), 0), BLK)
    seen = (key_at <= query_at) & (key_at < lengths_s[c])
    scores = jnp.where(seen, dot_nt(q4[...], kvb[0, 0, :BLK]) * SCALE, NEG_BIG)
    own_max = jnp.max(scores, axis=1, keepdims=True)
    weights = jnp.where(seen, jnp.exp(scores - own_max), 0.0)
    own_sum = jnp.sum(weights, axis=1, keepdims=True)
    own_value = dot_nn(weights.astype(BF16), kvb[0, 0, BLK:])

    n_q = NZ * HEADS * QROW
    lane = lax.broadcasted_iota(jnp.int32, (1, n_q), 1)
    reach = jnp.zeros((1, n_q), jnp.int32)
    for d in range(NZ):
        there = at(y, lax.rem(z + NZ - d, NZ), core) * QROW
        for r in range(QROW):
            spot = (lax.div(lane, HEADS * QROW) == d) & (lax.rem(lane, QROW) == r)
            reach = jnp.where(spot, positions_s[there + r], reach)

    for copy in kv_in:
        copy.wait_recv()
    sib_in = send(kvb.at[0], kvb.at[1], (at(y, z, 1 - core), g)) if NC > 1 else None
    wanted_z = jnp.zeros((2 * a_len, HEAD_DIM), jnp.int32) + anchor_z
    chosen = a2[0].astype(F32)
    for d in z_steps:
        a2_in[d].wait_recv()
        origin = lax.rem(z + NZ - d, NZ)
        chosen = jnp.where(wanted_z == origin, a2[d].astype(F32), chosen)
    anc[p] = chosen.astype(BF16)
    a3_in = [send(anc.at[p], anc.at[p], p_peer(dy, dc)) for dy, dc in p_steps]

    for copy in qz_in:
        copy.wait_recv()
    queries = qz[...].reshape(n_q, HEAD_DIM)
    if sib_in is not None:
        sib_in.wait_recv()
    blocks = []
    key_row = lax.broadcasted_iota(jnp.int32, (BLK, n_q), 0)
    part_max = jnp.full((1, n_q), NEG_BIG, F32)
    for k in range(NC):
        for d in range(NY):
            number = at(lax.rem(y + NY - d, NY), z, flip(k))
            visible = (key_row < lengths_s[number]) & (key_row + number * BLK <= reach)
            block_scores = dot_nt(kvb[k, d, :BLK], queries) * SCALE
            block_scores = jnp.where(visible, block_scores, NEG_BIG)
            part_max = jnp.maximum(part_max, jnp.max(block_scores, axis=0, keepdims=True))
            blocks.append((k, d, visible, block_scores))
    part_sum = jnp.zeros((1, n_q), F32)
    part_value = jnp.zeros((n_q, HEAD_DIM), F32)
    for k, d, visible, block_scores in blocks:
        block_weights = jnp.where(visible, jnp.exp(block_scores - part_max), 0.0)
        part_sum = part_sum + jnp.sum(block_weights, axis=0, keepdims=True)
        part_value = part_value + dot_tn(block_weights.astype(BF16), kvb[k, d, BLK:])
    n_r = HEADS * QROW
    stats = jnp.concatenate(
        split3(part_max) + split3(part_sum) + [jnp.zeros((10, n_q), F32)], axis=0
    ).astype(BF16)
    if n_q < LANES:
        stats = jnp.concatenate([stats, jnp.zeros((16, LANES - n_q), BF16)], axis=1)
    part[:, :n_r] = part_value.astype(BF16).reshape(NZ, n_r, HEAD_DIM)
    for d in range(NZ):
        group = d * n_r // LANES * LANES
        part[d, n_r:] = stats[:, group:group + LANES]
    part_ins = {NZ - d: send(part.at[d], part_in.at[NZ - d], z_peer(NZ - d)) for d in z_steps}

    for copy in a3_in:
        copy.wait_recv()
    a_keys = anc[:, :a_len].reshape(BLK, HEAD_DIM)
    a_values = anc[:, a_len:].reshape(BLK, HEAD_DIM)
    far = (key_at < lengths_s[anchor_block]) & (jnp.zeros_like(key_at) + anchor_block != c)
    scores = jnp.where(far, dot_nt(q4[...], a_keys) * SCALE, NEG_BIG)
    row_max = jnp.maximum(own_max, jnp.max(scores, axis=1, keepdims=True))
    weights = jnp.where(far, jnp.exp(scores - row_max), 0.0)
    own_factor = jnp.exp(own_max - row_max)
    total = jnp.sum(weights, axis=1, keepdims=True) + own_sum * own_factor
    value = dot_nn(weights.astype(BF16), a_values) + own_value * own_factor
    value = (value / total).astype(BF16)
    attended = jnp.concatenate([value[h * BLK:(h + 1) * BLK] for h in range(HEADS)], axis=1)

    def term(slot, j):
        return dot_nn(attended, w_out[slot, :, j * quarter:(j + 1) * quarter])

    wo_loads[3].wait()
    tr = {}
    for j in (0, 3, 1, 2):
        tr_out[j] = term(3, j).astype(BF16)
        tr[j] = send(tr_out.at[j], tr_in.at[j], right if j < 2 else left)
    wo_loads[2].wait()
    wo_loads[1].wait()
    final_r, final_l = {}, {}
    for j in (2, 3):
        to_right[j] = term(2, j).astype(BF16)
        final_r[j] = send(to_right.at[j], from_left.at[j], right)
        i = 3 - j
        to_left[i] = term(1, i).astype(BF16)
        final_l[i] = send(to_left.at[i], from_right.at[i], left)
    r_terms = {j: term(2, j) for j in (0, 1)}
    l_terms = {j: term(1, j) for j in (3, 2)}
    for j in (0, 1):
        tr[j].wait_recv()
        to_right[j] = (r_terms[j] + tr_in[j].astype(F32)).astype(BF16)
        final_r[j] = send(to_right.at[j], from_left.at[j], right)
        i = 3 - j
        tr[i].wait_recv()
        to_left[i] = (l_terms[i] + tr_in[i].astype(F32)).astype(BF16)
        final_l[i] = send(to_left.at[i], from_right.at[i], left)
    wo_loads[0].wait()
    own_term[...] = dot_nn(attended, w_out[0])

    eye_row = lax.broadcasted_iota(jnp.int32, (n_r, LANES), 0)
    eye_lane = lax.broadcasted_iota(jnp.int32, (n_r, LANES), 1)

    def column(rows, first, slot):
        line = rows[first:first + 1] + rows[first + 1:first + 2] + rows[first + 2:first + 3]
        spot = eye_lane == eye_row + (slot * n_r) % LANES
        return jnp.sum(jnp.where(spot, line, 0.0), axis=1, keepdims=True)

    maxima, sums, values = [], [], []
    for d in range(NZ):
        if d:
            part_ins[d].wait_recv()
        block = (part_in[d] if d else part[0]).astype(F32)
        slot = (NZ - d) % NZ
        maxima.append(column(block[n_r:], 0, slot))
        sums.append(column(block[n_r:], 3, slot))
        values.append(block[:n_r])
    top_max = maxima[0]
    for one in maxima[1:]:
        top_max = jnp.maximum(top_max, one)
    all_sum = jnp.zeros((n_r, 1), F32)
    all_value = jnp.zeros((n_r, HEAD_DIM), F32)
    for one_max, one_sum, one_value in zip(maxima, sums, values):
        factor = jnp.exp(one_max - top_max)
        all_sum = all_sum + one_sum * factor
        all_value = all_value + one_value * factor
    all_value = all_value / all_sum
    q_att = jnp.concatenate([all_value[h * QROW:(h + 1) * QROW] for h in range(HEADS)], axis=1)
    q_att = jnp.concatenate([q_att, jnp.zeros_like(q_att)], axis=0).astype(BF16)
    qx_in_copies = []
    for slot, device in ((3, opposite), (2, right), (1, left)):
        q_term = dot_nn(q_att, w_out[slot])[:QROW]
        qx_out[slot] = jnp.concatenate([q_term[:, :half_f], q_term[:, half_f:]], axis=0).astype(BF16)
        qx_in_copies.append(send(qx_out.at[slot], qx_in.at[slot], device))
    q_own = dot_nn(q_att, w_out[0])[:QROW]

    for j in (2, 1, 0, 3):
        final_r[j].wait_recv()
        final_l[j].wait_recv()
        columns = slice(j * quarter, (j + 1) * quarter)
        ctx_out[:, columns] = (
            own_term[:, columns] + from_left[j].astype(F32) + from_right[j].astype(F32)
        ).astype(BF16)
    for copy in qx_in_copies:
        copy.wait_recv()
    for slot in (1, 2, 3):
        packed = qx_in[slot].astype(F32)
        q_own = q_own + jnp.concatenate([packed[:QROW], packed[QROW:]], axis=1)
    q_out[...] = q_own.astype(BF16)
    for copy in copies:
        copy.wait_send()


def split3(x):
    high = x.astype(BF16).astype(F32)
    middle = (x - high).astype(BF16).astype(F32)
    return [high, middle, x - high - middle]


def local(tokens, questions, q_weight, k_weight, v_weight, o_weight, anchor, lengths, positions):
    n_r = HEADS * QROW
    n_p = NY * NC
    a_len = BLK // n_p
    anywhere = pl.BlockSpec(memory_space=pltpu.HBM)
    vmem = pl.BlockSpec(memory_space=pltpu.VMEM)
    smem = pl.BlockSpec(memory_space=pltpu.SMEM)
    operands = [
        pltpu.with_memory_space_constraint(x, pltpu.HBM)
        for x in (tokens, questions, q_weight, k_weight, v_weight, o_weight)
    ]
    lengths, positions = [
        pltpu.with_memory_space_constraint(x, pltpu.HBM) for x in (lengths, positions)
    ]
    return pl.pallas_call(
        kernel,
        out_shape=(
            jax.ShapeDtypeStruct((BLK, FEAT), BF16),
            jax.ShapeDtypeStruct((QROW, FEAT), BF16),
        ),
        in_specs=[anywhere] * 6 + [smem] + [anywhere] * 2,
        out_specs=(vmem, vmem),
        scratch_shapes=[
            pltpu.VMEM((QROW, FEAT), BF16),
            pltpu.SMEM(lengths.shape, jnp.int32),
            pltpu.SMEM(positions.shape, jnp.int32),
            pltpu.VMEM((NX, FEAT, WCOLS), BF16),
            pltpu.VMEM((NX, QCOLS, FEAT), BF16),
            pltpu.VMEM((BLK, FEAT), BF16),
            pltpu.VMEM((NX, 4, BLK, FEAT // 4), BF16),
            pltpu.VMEM((NX, 2 * QROW, FEAT // 2), BF16),
            pltpu.VMEM((BLK, WCOLS), F32),
            pltpu.VMEM((HEADS * BLK, HEAD_DIM), BF16),
            pltpu.VMEM((NZ, n_r, HEAD_DIM), BF16),
            pltpu.VMEM((NC, NY, 2 * BLK, HEAD_DIM), BF16),
            pltpu.VMEM((n_p, a_len, FEAT), BF16),
            pltpu.VMEM((NX, a_len, FEAT), BF16),
            pltpu.VMEM((NZ, 2 * a_len, HEAD_DIM), BF16),
            pltpu.VMEM((n_p, 2 * a_len, HEAD_DIM), BF16),
            pltpu.VMEM((NZ, n_r + 16, HEAD_DIM), BF16),
            pltpu.VMEM((NZ, n_r + 16, HEAD_DIM), BF16),
            pltpu.VMEM((4, BLK, FEAT // 4), BF16),
            pltpu.VMEM((4, BLK, FEAT // 4), BF16),
            pltpu.VMEM((4, BLK, FEAT // 4), BF16),
            pltpu.VMEM((4, BLK, FEAT // 4), BF16),
            pltpu.VMEM((4, BLK, FEAT // 4), BF16),
            pltpu.VMEM((4, BLK, FEAT // 4), BF16),
            pltpu.VMEM((BLK, FEAT), F32),
            pltpu.VMEM((NX, 2 * QROW, FEAT // 2), BF16),
            pltpu.VMEM((NX, 2 * QROW, FEAT // 2), BF16),
            pltpu.SemaphoreType.DMA((N_LOADS,)),
            pltpu.SemaphoreType.DMA((N_COPIES,)),
            pltpu.SemaphoreType.DMA((N_COPIES,)),
        ],
        compiler_params=pltpu.CompilerParams(
            collective_id=0, has_side_effects=True, vmem_limit_bytes=40 * 2**20
        ),
        name="fused_attention",
    )(*operands, anchor, lengths, positions)


def solution(mesh):
    in_specs = (
        P("ctx", "kvg"),
        P("ctx", "kvg"),
        P(None, "kvg"),
        P(None, "kvg"),
        P(None, "kvg"),
        P("kvg", None),
        P(),
        P(),
        P(),
    )
    out_specs = (P("ctx", "kvg"), P("ctx", "kvg"))
    return jax.shard_map(local, mesh=mesh, in_specs=in_specs, out_specs=out_specs, check_vma=False)
```

```python
import math

import jax
import jax.numpy as jnp
from jax import lax
from jax.experimental import pallas as pl
from jax.experimental.pallas import tpu as pltpu
from jax.sharding import PartitionSpec as P

HEAD_DIM = 128
NX = 4
NY, NZ, NC = 4, 8, 2
BLK = 128
QROW = 8
HEADS = 4
FEAT = 1024
QCOLS = HEADS * HEAD_DIM
WCOLS = QCOLS + 2 * HEAD_DIM
NEG_BIG = -1e30
SCALE = HEAD_DIM ** (-0.5)
F32 = jnp.float32
BF16 = jnp.bfloat16
MESH = pl.DeviceIdType.MESH
LANES = 128
N_COPIES = 96
N_LOADS = 20


def dot_nn(a, b):
    return jnp.dot(a, b, preferred_element_type=F32)


def dot_nt(a, b):
    return lax.dot_general(a, b, (((1,), (1,)), ((), ())), preferred_element_type=F32)


def dot_tn(a, b):
    return lax.dot_general(a, b, (((0,), (0,)), ((), ())), preferred_element_type=F32)


def angles(places):
    lane = lax.broadcasted_iota(jnp.int32, places.shape, 1)
    half = HEAD_DIM // 2
    index = jnp.where(lane < half, lane, lane - half).astype(F32)
    frequency = jnp.exp(index * (-2.0 * math.log(500000.0) / HEAD_DIM))
    angle = places.astype(F32) * frequency
    sine = jnp.sin(angle)
    return jnp.cos(angle), jnp.where(lane < half, -sine, sine)


def rotate(head, cosine, sine):
    return head * cosine + pltpu.roll(head, HEAD_DIM // 2, 1) * sine


def kernel(
    tokens, questions, wq, wk, wv, wo, anchor, lengths, positions,
    ctx_out, q_out,
    asked, lengths_s, positions_s, w_in, w_out, own_tok, tok, qpack, acc, q4, qz, kvb,
    a_rows, a_tok, a2, anc, part, part_in, tr_out, tr_in, to_right, to_left,
    from_left, from_right, own_term, qx_out, qx_in, load_sem, send_sem, recv_sem,
):
    n_p = NY * NC
    a_len = BLK // n_p
    c = lax.axis_index("ctx")
    g = lax.axis_index("kvg")
    core = lax.rem(c, NC)
    z = lax.rem(lax.div(c, NC), NZ)
    y = lax.div(c, NC * NZ)
    p = y * NC + core

    def at(y_, z_, core_):
        return (y_ * NZ + z_) * NC + core_

    src = [g, lax.rem(g + 3, NX), lax.rem(g + 1, NX), lax.rem(g + 2, NX)]
    left, right, opposite = (c, src[1]), (c, src[2]), (c, src[3])

    def flip(dc):
        return 1 - core if dc else core

    p_steps = [(dy, dc) for dy in range(NY) for dc in range(NC) if dy or dc]
    p_steps.sort(key=lambda s: (-min(s[0], NY - s[0]), -s[1]))
    z_steps = sorted(range(1, NZ), key=lambda d: -min(d, NZ - d))

    def p_peer(dy, dc):
        return (at(lax.rem(y + dy, NY), z, flip(dc)), g)

    def p_index(dy, dc):
        return lax.rem(y + dy, NY) * NC + flip(dc)

    def z_peer(d):
        return (at(y, lax.rem(z + d, NZ), core), g)

    partners = [z_peer(d) for d in z_steps] + [opposite]
    partners += [p_peer(dy, dc) for dy, dc in p_steps] + [left, right]
    barrier = pltpu.get_barrier_semaphore()
    for partner in partners:
        pl.semaphore_signal(barrier, inc=1, device_id=partner, device_id_type=MESH)

    loads = []

    def load(source, target):
        copy = pltpu.make_async_copy(source, target, load_sem.at[len(loads)])
        copy.start()
        loads.append(copy)
        return copy

    asked_load = load(questions, asked)
    scalar_loads = [load(lengths, lengths_s), load(positions, positions_s)]
    tok_load = load(tokens, own_tok)
    w_loads = []
    for slot in range(NX):
        rows = pl.ds(pl.multiple_of(src[slot] * FEAT, FEAT), FEAT)
        w_loads.append([
            load(wq.at[rows, :], w_in.at[slot, :, pl.ds(0, QCOLS)]),
            load(wk.at[rows, :], w_in.at[slot, :, pl.ds(QCOLS, HEAD_DIM)]),
            load(wv.at[rows, :], w_in.at[slot, :, pl.ds(QCOLS + HEAD_DIM, HEAD_DIM)]),
        ])

    asked_load.wait()
    own_questions = asked[...].astype(F32)
    half_f = FEAT // 2
    qpack[0] = jnp.concatenate(
        [own_questions[:, :half_f], own_questions[:, half_f:]], axis=0
    ).astype(BF16)
    pl.semaphore_wait(barrier, len(partners))

    copies = []

    def send(source, target, device):
        index = len(copies)
        copy = pltpu.make_async_remote_copy(
            src_ref=source, dst_ref=target, send_sem=send_sem.at[index],
            recv_sem=recv_sem.at[index], device_id=device, device_id_type=MESH,
        )
        copy.start()
        copies.append(copy)
        return copy

    quarter = FEAT // 4
    near_r, near_l = {}, {}

    def send_tokens(j_r, j_l):
        near_r[j_r] = send(tokens.at[:, pl.ds(j_r * quarter, quarter)], tok.at[1, j_r], right)
        near_l[j_l] = send(tokens.at[:, pl.ds(j_l * quarter, quarter)], tok.at[2, j_l], left)

    send_tokens(0, 3)
    a_in = {}
    for dy, dc in p_steps:
        there = pl.ds(pl.multiple_of(p_index(dy, dc) * a_len, a_len), a_len)
        a_in[dy, dc] = send(tokens.at[there, :], a_rows.at[dy * NC + dc], p_peer(dy, dc))
    send_tokens(1, 2)

    tok_load.wait()
    for copy in w_loads[0]:
        copy.wait()
    acc[...] = dot_nn(own_tok[...], w_in[0])
    row = lax.broadcasted_iota(jnp.int32, (BLK, HEAD_DIM), 0)
    cosine, sine = angles(row + c * BLK)
    send_tokens(2, 1)
    for copy in scalar_loads:
        copy.wait()
    q_row = lax.broadcasted_iota(jnp.int32, (QROW, HEAD_DIM), 0)
    q_places = jnp.zeros((QROW, HEAD_DIM), jnp.int32)
    for r in range(QROW):
        q_places = jnp.where(q_row == r, positions_s[c * QROW + r], q_places)
    q_cosine, q_sine = angles(q_places)
    anchor_block = anchor[0]
    anchor_y = lax.div(anchor_block, NC * NZ)
    anchor_core = lax.rem(anchor_block, NC)
    anchor_z = lax.rem(lax.div(anchor_block, NC), NZ)
    a_row = lax.broadcasted_iota(jnp.int32, (a_len, HEAD_DIM), 0)
    a_cosine, a_sine = angles(a_row + p * a_len + anchor_block * BLK)
    send_tokens(3, 0)

    n_q = NZ * HEADS * QROW
    lane = lax.broadcasted_iota(jnp.int32, (1, n_q), 1)
    reach = jnp.zeros((1, n_q), jnp.int32)
    for d in range(NZ):
        there = at(y, lax.rem(z + NZ - d, NZ), core) * QROW
        for r in range(QROW):
            spot = (lax.div(lane, HEADS * QROW) == d) & (lax.rem(lane, QROW) == r)
            reach = jnp.where(spot, positions_s[there + r], reach)

    wanted = jnp.zeros((a_len, FEAT), jnp.int32)
    wanted_p = wanted + (anchor_y * NC + anchor_core)
    chosen = own_tok[pl.ds(pl.multiple_of(p * a_len, a_len), a_len), :].astype(F32)
    for dy, dc in p_steps:
        a_in[dy, dc].wait_recv()
        origin = lax.rem(y + NY - dy, NY) * NC + flip(dc)
        chosen = jnp.where(wanted_p == origin, a_rows[dy * NC + dc].astype(F32), chosen)
    a_tok[0] = chosen.astype(BF16)
    at_in = [
        send(a_tok.at[0], a_tok.at[3], opposite),
        send(a_tok.at[0], a_tok.at[1], right),
        send(a_tok.at[0], a_tok.at[2], left),
    ]

    far_r, far_l = {}, {}

    def pass_on(j_r, j_l):
        near_r[j_r].wait_recv()
        far_r[j_r] = send(tok.at[1, j_r], tok.at[3, j_r], right)
        near_l[j_l].wait_recv()
        far_l[j_l] = send(tok.at[2, j_l], tok.at[3, j_l], left)

    pass_on(0, 3)
    pass_on(1, 2)
    q_in = [
        send(qpack.at[0], qpack.at[3], opposite),
        send(qpack.at[0], qpack.at[1], right),
        send(qpack.at[0], qpack.at[2], left),
    ]

    for slot in (1, 2):
        for copy in w_loads[slot]:
            copy.wait()
    for j in range(2):
        acc[...] += dot_nn(tok[1, j], w_in[1, j * quarter:(j + 1) * quarter])
        k = 3 - j
        acc[...] += dot_nn(tok[2, k], w_in[2, k * quarter:(k + 1) * quarter])
    for copy in w_loads[3]:
        copy.wait()
    for copy in at_in:
        copy.wait_recv()
    a_kv = jnp.zeros((a_len, 2 * HEAD_DIM), F32)
    for slot in range(NX):
        a_kv = a_kv + dot_nn(a_tok[slot], w_in[slot, :, QCOLS:])
    a2[0, :a_len] = rotate(a_kv[:, :HEAD_DIM], a_cosine, a_sine).astype(BF16)
    a2[0, a_len:] = a_kv[:, HEAD_DIM:].astype(BF16)
    a2_in = {d: send(a2.at[0], a2.at[d], z_peer(d)) for d in z_steps}
    wo_loads = {}
    for slot in (3, 2, 1, 0):
        columns = pl.ds(pl.multiple_of(src[slot] * FEAT, FEAT), FEAT)
        wo_loads[slot] = load(wo.at[:, columns], w_out.at[slot])

    for j in range(2, 4):
        near_r[j].wait_recv()
        acc[...] += dot_nn(tok[1, j], w_in[1, j * quarter:(j + 1) * quarter])
        k = 3 - j
        near_l[k].wait_recv()
        acc[...] += dot_nn(tok[2, k], w_in[2, k * quarter:(k + 1) * quarter])

    for j in (0, 3, 1):
        (far_r if j < 2 else far_l)[j].wait_recv()
        acc[...] += dot_nn(tok[3, j], w_in[3, j * quarter:(j + 1) * quarter])
    far_l[2].wait_recv()
    last_rows = slice(2 * quarter, 3 * quarter)
    key_value = acc[:, QCOLS:] + dot_nn(tok[3, 2], w_in[3, last_rows, QCOLS:])
    kvb[0, 0, :BLK] = rotate(key_value[:, :HEAD_DIM], cosine, sine).astype(BF16)
    kvb[0, 0, BLK:] = key_value[:, HEAD_DIM:].astype(BF16)
    kv_in = [
        send(kvb.at[0, 0], kvb.at[0, d], p_peer(d, 0))
        for d in sorted(range(1, NY), key=lambda d: -min(d, NY - d))
    ]

    for copy in q_in:
        copy.wait_recv()
    q_total = jnp.zeros((2 * QROW, QCOLS), F32)
    for slot in range(NX):
        packed = qpack[slot].astype(F32)
        rows = jnp.concatenate([packed[:QROW], packed[QROW:]], axis=1)
        rows = jnp.concatenate([rows, jnp.zeros_like(rows)], axis=0).astype(BF16)
        q_total = q_total + dot_nn(rows, w_in[slot, :, :QCOLS])
    q_heads = [
        rotate(q_total[:QROW, h * HEAD_DIM:(h + 1) * HEAD_DIM], q_cosine, q_sine)
        for h in range(HEADS)
    ]
    qz[0] = jnp.concatenate(q_heads, axis=0).astype(BF16)
    qz_in = [send(qz.at[0], qz.at[d], z_peer(d)) for d in z_steps]

    wanted_z = jnp.zeros((2 * a_len, HEAD_DIM), jnp.int32) + anchor_z
    chosen = a2[0].astype(F32)
    for d in z_steps:
        a2_in[d].wait_recv()
        origin = lax.rem(z + NZ - d, NZ)
        chosen = jnp.where(wanted_z == origin, a2[d].astype(F32), chosen)
    anc[p] = chosen.astype(BF16)
    a3_in = [send(anc.at[p], anc.at[p], p_peer(dy, dc)) for dy, dc in p_steps]

    query = acc[:, :QCOLS] + dot_nn(tok[3, 2], w_in[3, last_rows, :QCOLS])
    for h in range(HEADS):
        head = query[:, h * HEAD_DIM:(h + 1) * HEAD_DIM]
        q4[h * BLK:(h + 1) * BLK] = rotate(head, cosine, sine).astype(BF16)
    key_at = lax.broadcasted_iota(jnp.int32, (HEADS * BLK, BLK), 1)
    query_at = lax.rem(lax.broadcasted_iota(jnp.int32, (HEADS * BLK, BLK), 0), BLK)
    seen = (key_at <= query_at) & (key_at < lengths_s[c])
    scores = jnp.where(seen, dot_nt(q4[...], kvb[0, 0, :BLK]) * SCALE, NEG_BIG)
    own_max = jnp.max(scores, axis=1, keepdims=True)
    weights = jnp.where(seen, jnp.exp(scores - own_max), 0.0)
    own_sum = jnp.sum(weights, axis=1, keepdims=True)
    own_value = dot_nn(weights.astype(BF16), kvb[0, 0, BLK:])

    done = len(copies)
    for copy in copies[:done - len(a3_in)]:
        copy.wait_send()
    done -= len(a3_in)

    for copy in a3_in:
        copy.wait_recv()
    a_keys = anc[:, :a_len].reshape(BLK, HEAD_DIM)
    a_values = anc[:, a_len:].reshape(BLK, HEAD_DIM)
    far = (key_at < lengths_s[anchor_block]) & (jnp.zeros_like(key_at) + anchor_block != c)
    scores = jnp.where(far, dot_nt(q4[...], a_keys) * SCALE, NEG_BIG)
    row_max = jnp.maximum(own_max, jnp.max(scores, axis=1, keepdims=True))
    weights = jnp.where(far, jnp.exp(scores - row_max), 0.0)
    own_factor = jnp.exp(own_max - row_max)
    total = jnp.sum(weights, axis=1, keepdims=True) + own_sum * own_factor
    value = dot_nn(weights.astype(BF16), a_values) + own_value * own_factor
    value = (value / total).astype(BF16)
    attended = jnp.concatenate([value[h * BLK:(h + 1) * BLK] for h in range(HEADS)], axis=1)

    def term(slot, j):
        return dot_nn(attended, w_out[slot, :, j * quarter:(j + 1) * quarter])

    wo_loads[3].wait()
    tr = {}
    for j in (0, 3, 1, 2):
        tr_out[j] = term(3, j).astype(BF16)
        tr[j] = send(tr_out.at[j], tr_in.at[j], right if j < 2 else left)
    for copy in kv_in:
        copy.wait_recv()
    sib_in = send(kvb.at[0], kvb.at[1], (at(y, z, 1 - core), g)) if NC > 1 else None
    wo_loads[2].wait()
    wo_loads[1].wait()
    final_r, final_l = {}, {}
    for j in (2, 3):
        to_right[j] = term(2, j).astype(BF16)
        final_r[j] = send(to_right.at[j], from_left.at[j], right)
        i = 3 - j
        to_left[i] = term(1, i).astype(BF16)
        final_l[i] = send(to_left.at[i], from_right.at[i], left)
    r_terms = {j: term(2, j) for j in (0, 1)}
    l_terms = {j: term(1, j) for j in (3, 2)}

    for copy in qz_in:
        copy.wait_recv()
    queries = qz[...].reshape(n_q, HEAD_DIM)
    if sib_in is not None:
        sib_in.wait_recv()
    blocks = []
    key_row = lax.broadcasted_iota(jnp.int32, (BLK, n_q), 0)
    part_max = jnp.full((1, n_q), NEG_BIG, F32)
    for k in range(NC):
        for d in range(NY):
            number = at(lax.rem(y + NY - d, NY), z, flip(k))
            visible = (key_row < lengths_s[number]) & (key_row + number * BLK <= reach)
            block_scores = dot_nt(kvb[k, d, :BLK], queries) * SCALE
            block_scores = jnp.where(visible, block_scores, NEG_BIG)
            part_max = jnp.maximum(part_max, jnp.max(block_scores, axis=0, keepdims=True))
            blocks.append((k, d, visible, block_scores))
    part_sum = jnp.zeros((1, n_q), F32)
    part_value = jnp.zeros((n_q, HEAD_DIM), F32)
    for k, d, visible, block_scores in blocks:
        block_weights = jnp.where(visible, jnp.exp(block_scores - part_max), 0.0)
        part_sum = part_sum + jnp.sum(block_weights, axis=0, keepdims=True)
        part_value = part_value + dot_tn(block_weights.astype(BF16), kvb[k, d, BLK:])
    n_r = HEADS * QROW
    stats = jnp.concatenate(
        split3(part_max) + split3(part_sum) + [jnp.zeros((10, n_q), F32)], axis=0
    ).astype(BF16)
    if n_q < LANES:
        stats = jnp.concatenate([stats, jnp.zeros((16, LANES - n_q), BF16)], axis=1)
    part[:, :n_r] = part_value.astype(BF16).reshape(NZ, n_r, HEAD_DIM)
    for d in range(NZ):
        group = d * n_r // LANES * LANES
        part[d, n_r:] = stats[:, group:group + LANES]
    part_ins = {NZ - d: send(part.at[d], part_in.at[NZ - d], z_peer(NZ - d)) for d in z_steps}

    for j in (0, 1):
        tr[j].wait_recv()
        to_right[j] = (r_terms[j] + tr_in[j].astype(F32)).astype(BF16)
        final_r[j] = send(to_right.at[j], from_left.at[j], right)
        i = 3 - j
        tr[i].wait_recv()
        to_left[i] = (l_terms[i] + tr_in[i].astype(F32)).astype(BF16)
        final_l[i] = send(to_left.at[i], from_right.at[i], left)
    wo_loads[0].wait()
    own_term[...] = dot_nn(attended, w_out[0])

    eye_row = lax.broadcasted_iota(jnp.int32, (n_r, LANES), 0)
    eye_lane = lax.broadcasted_iota(jnp.int32, (n_r, LANES), 1)

    def column(rows, first, slot):
        line = rows[first:first + 1] + rows[first + 1:first + 2] + rows[first + 2:first + 3]
        spot = eye_lane == eye_row + (slot * n_r) % LANES
        return jnp.sum(jnp.where(spot, line, 0.0), axis=1, keepdims=True)

    maxima, sums, values = [], [], []
    for d in range(NZ):
        if d:
            part_ins[d].wait_recv()
        block = (part_in[d] if d else part[0]).astype(F32)
        slot = (NZ - d) % NZ
        maxima.append(column(block[n_r:], 0, slot))
        sums.append(column(block[n_r:], 3, slot))
        values.append(block[:n_r])
    top_max = maxima[0]
    for one in maxima[1:]:
        top_max = jnp.maximum(top_max, one)
    all_sum = jnp.zeros((n_r, 1), F32)
    all_value = jnp.zeros((n_r, HEAD_DIM), F32)
    for one_max, one_sum, one_value in zip(maxima, sums, values):
        factor = jnp.exp(one_max - top_max)
        all_sum = all_sum + one_sum * factor
        all_value = all_value + one_value * factor
    all_value = all_value / all_sum
    q_att = jnp.concatenate([all_value[h * QROW:(h + 1) * QROW] for h in range(HEADS)], axis=1)
    q_att = jnp.concatenate([q_att, jnp.zeros_like(q_att)], axis=0).astype(BF16)
    qx_in_copies = []
    for slot, device in ((3, opposite), (2, right), (1, left)):
        q_term = dot_nn(q_att, w_out[slot])[:QROW]
        qx_out[slot] = jnp.concatenate([q_term[:, :half_f], q_term[:, half_f:]], axis=0).astype(BF16)
        qx_in_copies.append(send(qx_out.at[slot], qx_in.at[slot], device))
    q_own = dot_nn(q_att, w_out[0])[:QROW]

    for j in (2, 1, 0, 3):
        final_r[j].wait_recv()
        final_l[j].wait_recv()
        columns = slice(j * quarter, (j + 1) * quarter)
        ctx_out[:, columns] = (
            own_term[:, columns] + from_left[j].astype(F32) + from_right[j].astype(F32)
        ).astype(BF16)
    for copy in qx_in_copies:
        copy.wait_recv()
    for slot in (1, 2, 3):
        packed = qx_in[slot].astype(F32)
        q_own = q_own + jnp.concatenate([packed[:QROW], packed[QROW:]], axis=1)
    q_out[...] = q_own.astype(BF16)
    for copy in copies[done:]:
        copy.wait_send()


def split3(x):
    high = x.astype(BF16).astype(F32)
    middle = (x - high).astype(BF16).astype(F32)
    return [high, middle, x - high - middle]


def local(tokens, questions, q_weight, k_weight, v_weight, o_weight, anchor, lengths, positions):
    n_r = HEADS * QROW
    n_p = NY * NC
    a_len = BLK // n_p
    anywhere = pl.BlockSpec(memory_space=pltpu.HBM)
    vmem = pl.BlockSpec(memory_space=pltpu.VMEM)
    smem = pl.BlockSpec(memory_space=pltpu.SMEM)
    operands = [
        pltpu.with_memory_space_constraint(x, pltpu.HBM)
        for x in (tokens, questions, q_weight, k_weight, v_weight, o_weight)
    ]
    lengths, positions = [
        pltpu.with_memory_space_constraint(x, pltpu.HBM) for x in (lengths, positions)
    ]
    return pl.pallas_call(
        kernel,
        out_shape=(
            jax.ShapeDtypeStruct((BLK, FEAT), BF16),
            jax.ShapeDtypeStruct((QROW, FEAT), BF16),
        ),
        in_specs=[anywhere] * 6 + [smem] + [anywhere] * 2,
        out_specs=(vmem, vmem),
        scratch_shapes=[
            pltpu.VMEM((QROW, FEAT), BF16),
            pltpu.SMEM(lengths.shape, jnp.int32),
            pltpu.SMEM(positions.shape, jnp.int32),
            pltpu.VMEM((NX, FEAT, WCOLS), BF16),
            pltpu.VMEM((NX, QCOLS, FEAT), BF16),
            pltpu.VMEM((BLK, FEAT), BF16),
            pltpu.VMEM((NX, 4, BLK, FEAT // 4), BF16),
            pltpu.VMEM((NX, 2 * QROW, FEAT // 2), BF16),
            pltpu.VMEM((BLK, WCOLS), F32),
            pltpu.VMEM((HEADS * BLK, HEAD_DIM), BF16),
            pltpu.VMEM((NZ, n_r, HEAD_DIM), BF16),
            pltpu.VMEM((NC, NY, 2 * BLK, HEAD_DIM), BF16),
            pltpu.VMEM((n_p, a_len, FEAT), BF16),
            pltpu.VMEM((NX, a_len, FEAT), BF16),
            pltpu.VMEM((NZ, 2 * a_len, HEAD_DIM), BF16),
            pltpu.VMEM((n_p, 2 * a_len, HEAD_DIM), BF16),
            pltpu.VMEM((NZ, n_r + 16, HEAD_DIM), BF16),
            pltpu.VMEM((NZ, n_r + 16, HEAD_DIM), BF16),
            pltpu.VMEM((4, BLK, FEAT // 4), BF16),
            pltpu.VMEM((4, BLK, FEAT // 4), BF16),
            pltpu.VMEM((4, BLK, FEAT // 4), BF16),
            pltpu.VMEM((4, BLK, FEAT // 4), BF16),
            pltpu.VMEM((4, BLK, FEAT // 4), BF16),
            pltpu.VMEM((4, BLK, FEAT // 4), BF16),
            pltpu.VMEM((BLK, FEAT), F32),
            pltpu.VMEM((NX, 2 * QROW, FEAT // 2), BF16),
            pltpu.VMEM((NX, 2 * QROW, FEAT // 2), BF16),
            pltpu.SemaphoreType.DMA((N_LOADS,)),
            pltpu.SemaphoreType.DMA((N_COPIES,)),
            pltpu.SemaphoreType.DMA((N_COPIES,)),
        ],
        compiler_params=pltpu.CompilerParams(
            collective_id=0, has_side_effects=True, vmem_limit_bytes=40 * 2**20
        ),
        name="fused_attention",
    )(*operands, anchor, lengths, positions)


def solution(mesh):
    in_specs = (
        P("ctx", "kvg"),
        P("ctx", "kvg"),
        P(None, "kvg"),
        P(None, "kvg"),
        P(None, "kvg"),
        P("kvg", None),
        P(),
        P(),
        P(),
    )
    out_specs = (P("ctx", "kvg"), P("ctx", "kvg"))
    return jax.shard_map(local, mesh=mesh, in_specs=in_specs, out_specs=out_specs, check_vma=False)
```

```python
import math

import jax
import jax.numpy as jnp
from jax import lax
from jax.experimental import pallas as pl
from jax.experimental.pallas import tpu as pltpu
from jax.sharding import PartitionSpec as P

HEAD_DIM = 128
NX = 4
NY, NZ, NC = 4, 8, 2
BLK = 128
QROW = 8
HEADS = 4
FEAT = 1024
QCOLS = HEADS * HEAD_DIM
WCOLS = QCOLS + 2 * HEAD_DIM
NEG_BIG = -1e30
SCALE = HEAD_DIM ** (-0.5)
F32 = jnp.float32
BF16 = jnp.bfloat16
MESH = pl.DeviceIdType.MESH
LANES = 128
N_COPIES = 96
N_LOADS = 20


def dot_nn(a, b):
    return jnp.dot(a, b, preferred_element_type=F32)


def dot_nt(a, b):
    return lax.dot_general(a, b, (((1,), (1,)), ((), ())), preferred_element_type=F32)


def dot_tn(a, b):
    return lax.dot_general(a, b, (((0,), (0,)), ((), ())), preferred_element_type=F32)


def angles(places):
    lane = lax.broadcasted_iota(jnp.int32, places.shape, 1)
    half = HEAD_DIM // 2
    index = jnp.where(lane < half, lane, lane - half).astype(F32)
    frequency = jnp.exp(index * (-2.0 * math.log(500000.0) / HEAD_DIM))
    angle = places.astype(F32) * frequency
    sine = jnp.sin(angle)
    return jnp.cos(angle), jnp.where(lane < half, -sine, sine)


def rotate(head, cosine, sine):
    return head * cosine + pltpu.roll(head, HEAD_DIM // 2, 1) * sine


def kernel(
    tokens, questions, wq, wk, wv, wo, anchor, lengths, positions,
    ctx_out, q_out,
    asked, lengths_s, positions_s, w_in, w_out, own_tok, tok, qpack, acc, q4, qz, kvb,
    a_rows, a_tok, a2, anc, part, part_in, tr_out, tr_in, to_right, to_left,
    from_left, from_right, own_term, qx_out, qx_in, load_sem, send_sem, recv_sem,
):
    n_p = NY * NC
    a_len = BLK // n_p
    c = lax.axis_index("ctx")
    g = lax.axis_index("kvg")
    core = lax.rem(c, NC)
    z = lax.rem(lax.div(c, NC), NZ)
    y = lax.div(c, NC * NZ)
    p = y * NC + core

    def at(y_, z_, core_):
        return (y_ * NZ + z_) * NC + core_

    src = [g, lax.rem(g + 3, NX), lax.rem(g + 1, NX), lax.rem(g + 2, NX)]
    left, right, opposite = (c, src[1]), (c, src[2]), (c, src[3])

    def flip(dc):
        return 1 - core if dc else core

    p_steps = [(dy, dc) for dy in range(NY) for dc in range(NC) if dy or dc]
    p_steps.sort(key=lambda s: (-min(s[0], NY - s[0]), -s[1]))
    z_steps = sorted(range(1, NZ), key=lambda d: -min(d, NZ - d))

    def p_peer(dy, dc):
        return (at(lax.rem(y + dy, NY), z, flip(dc)), g)

    def p_index(dy, dc):
        return lax.rem(y + dy, NY) * NC + flip(dc)

    def z_peer(d):
        return (at(y, lax.rem(z + d, NZ), core), g)

    partners = [z_peer(d) for d in z_steps] + [opposite]
    partners += [p_peer(dy, dc) for dy, dc in p_steps] + [left, right]
    barrier = pltpu.get_barrier_semaphore()
    for partner in partners:
        pl.semaphore_signal(barrier, inc=1, device_id=partner, device_id_type=MESH)

    loads = []

    def load(source, target):
        copy = pltpu.make_async_copy(source, target, load_sem.at[len(loads)])
        copy.start()
        loads.append(copy)
        return copy

    asked_load = load(questions, asked)
    scalar_loads = [load(lengths, lengths_s), load(positions, positions_s)]
    tok_load = load(tokens, own_tok)
    w_loads = []
    for slot in range(NX):
        rows = pl.ds(pl.multiple_of(src[slot] * FEAT, FEAT), FEAT)
        w_loads.append([
            load(wq.at[rows, :], w_in.at[slot, :, pl.ds(0, QCOLS)]),
            load(wk.at[rows, :], w_in.at[slot, :, pl.ds(QCOLS, HEAD_DIM)]),
            load(wv.at[rows, :], w_in.at[slot, :, pl.ds(QCOLS + HEAD_DIM, HEAD_DIM)]),
        ])

    asked_load.wait()
    own_questions = asked[...].astype(F32)
    half_f = FEAT // 2
    qpack[0] = jnp.concatenate(
        [own_questions[:, :half_f], own_questions[:, half_f:]], axis=0
    ).astype(BF16)
    pl.semaphore_wait(barrier, len(partners))

    copies = []

    def send(source, target, device):
        index = len(copies)
        copy = pltpu.make_async_remote_copy(
            src_ref=source, dst_ref=target, send_sem=send_sem.at[index],
            recv_sem=recv_sem.at[index], device_id=device, device_id_type=MESH,
        )
        copy.start()
        copies.append(copy)
        return copy

    quarter = FEAT // 4
    near_r, near_l = {}, {}

    def send_tokens(j_r, j_l):
        near_r[j_r] = send(tokens.at[:, pl.ds(j_r * quarter, quarter)], tok.at[1, j_r], right)
        near_l[j_l] = send(tokens.at[:, pl.ds(j_l * quarter, quarter)], tok.at[2, j_l], left)

    send_tokens(0, 3)
    a_in = {}
    for dy, dc in p_steps:
        there = pl.ds(pl.multiple_of(p_index(dy, dc) * a_len, a_len), a_len)
        a_in[dy, dc] = send(tokens.at[there, :], a_rows.at[dy * NC + dc], p_peer(dy, dc))
    send_tokens(1, 2)

    tok_load.wait()
    for copy in w_loads[0]:
        copy.wait()
    acc[...] = dot_nn(own_tok[...], w_in[0])
    row = lax.broadcasted_iota(jnp.int32, (BLK, HEAD_DIM), 0)
    cosine, sine = angles(row + c * BLK)
    send_tokens(2, 1)
    for copy in scalar_loads:
        copy.wait()
    q_row = lax.broadcasted_iota(jnp.int32, (QROW, HEAD_DIM), 0)
    q_places = jnp.zeros((QROW, HEAD_DIM), jnp.int32)
    for r in range(QROW):
        q_places = jnp.where(q_row == r, positions_s[c * QROW + r], q_places)
    q_cosine, q_sine = angles(q_places)
    anchor_block = anchor[0]
    anchor_y = lax.div(anchor_block, NC * NZ)
    anchor_core = lax.rem(anchor_block, NC)
    anchor_z = lax.rem(lax.div(anchor_block, NC), NZ)
    a_row = lax.broadcasted_iota(jnp.int32, (a_len, HEAD_DIM), 0)
    a_cosine, a_sine = angles(a_row + p * a_len + anchor_block * BLK)

    n_q = NZ * HEADS * QROW
    lane = lax.broadcasted_iota(jnp.int32, (1, n_q), 1)
    reach = jnp.zeros((1, n_q), jnp.int32)
    for d in range(NZ):
        there = at(y, lax.rem(z + NZ - d, NZ), core) * QROW
        for r in range(QROW):
            spot = (lax.div(lane, HEADS * QROW) == d) & (lax.rem(lane, QROW) == r)
            reach = jnp.where(spot, positions_s[there + r], reach)

    wanted = jnp.zeros((a_len, FEAT), jnp.int32)
    wanted_p = wanted + (anchor_y * NC + anchor_core)
    chosen = own_tok[pl.ds(pl.multiple_of(p * a_len, a_len), a_len), :].astype(F32)
    for dy, dc in p_steps:
        a_in[dy, dc].wait_recv()
        origin = lax.rem(y + NY - dy, NY) * NC + flip(dc)
        chosen = jnp.where(wanted_p == origin, a_rows[dy * NC + dc].astype(F32), chosen)
    a_tok[0] = chosen.astype(BF16)
    at_in = [
        send(a_tok.at[0], a_tok.at[3], opposite),
        send(a_tok.at[0], a_tok.at[1], right),
        send(a_tok.at[0], a_tok.at[2], left),
    ]

    send_tokens(3, 0)

    far_r, far_l = {}, {}

    def pass_on(j_r, j_l):
        near_r[j_r].wait_recv()
        far_r[j_r] = send(tok.at[1, j_r], tok.at[3, j_r], right)
        near_l[j_l].wait_recv()
        far_l[j_l] = send(tok.at[2, j_l], tok.at[3, j_l], left)

    pass_on(0, 3)
    pass_on(1, 2)
    q_in = [
        send(qpack.at[0], qpack.at[3], opposite),
        send(qpack.at[0], qpack.at[1], right),
        send(qpack.at[0], qpack.at[2], left),
    ]

    for slot in (1, 2):
        for copy in w_loads[slot]:
            copy.wait()
    for j in range(2):
        acc[...] += dot_nn(tok[1, j], w_in[1, j * quarter:(j + 1) * quarter])
        k = 3 - j
        acc[...] += dot_nn(tok[2, k], w_in[2, k * quarter:(k + 1) * quarter])
    for copy in w_loads[3]:
        copy.wait()
    for copy in at_in:
        copy.wait_recv()
    a_kv = jnp.zeros((a_len, 2 * HEAD_DIM), F32)
    for slot in range(NX):
        a_kv = a_kv + dot_nn(a_tok[slot], w_in[slot, :, QCOLS:])
    a2[0, :a_len] = rotate(a_kv[:, :HEAD_DIM], a_cosine, a_sine).astype(BF16)
    a2[0, a_len:] = a_kv[:, HEAD_DIM:].astype(BF16)
    a2_in = {d: send(a2.at[0], a2.at[d], z_peer(d)) for d in z_steps}
    wo_loads = {}
    for slot in (3, 2, 1, 0):
        columns = pl.ds(pl.multiple_of(src[slot] * FEAT, FEAT), FEAT)
        wo_loads[slot] = load(wo.at[:, columns], w_out.at[slot])

    for j in range(2, 4):
        near_r[j].wait_recv()
        acc[...] += dot_nn(tok[1, j], w_in[1, j * quarter:(j + 1) * quarter])
        k = 3 - j
        near_l[k].wait_recv()
        acc[...] += dot_nn(tok[2, k], w_in[2, k * quarter:(k + 1) * quarter])

    for j in (0, 3, 1):
        (far_r if j < 2 else far_l)[j].wait_recv()
        acc[...] += dot_nn(tok[3, j], w_in[3, j * quarter:(j + 1) * quarter])
    far_l[2].wait_recv()
    last_rows = slice(2 * quarter, 3 * quarter)
    key_value = acc[:, QCOLS:] + dot_nn(tok[3, 2], w_in[3, last_rows, QCOLS:])
    kvb[0, 0, :BLK] = rotate(key_value[:, :HEAD_DIM], cosine, sine).astype(BF16)
    kvb[0, 0, BLK:] = key_value[:, HEAD_DIM:].astype(BF16)
    kv_in = [
        send(kvb.at[0, 0], kvb.at[0, d], p_peer(d, 0))
        for d in sorted(range(1, NY), key=lambda d: -min(d, NY - d))
    ]

    for copy in q_in:
        copy.wait_recv()
    q_total = jnp.zeros((2 * QROW, QCOLS), F32)
    for slot in range(NX):
        packed = qpack[slot].astype(F32)
        rows = jnp.concatenate([packed[:QROW], packed[QROW:]], axis=1)
        rows = jnp.concatenate([rows, jnp.zeros_like(rows)], axis=0).astype(BF16)
        q_total = q_total + dot_nn(rows, w_in[slot, :, :QCOLS])
    q_heads = [
        rotate(q_total[:QROW, h * HEAD_DIM:(h + 1) * HEAD_DIM], q_cosine, q_sine)
        for h in range(HEADS)
    ]
    qz[0] = jnp.concatenate(q_heads, axis=0).astype(BF16)
    qz_in = [send(qz.at[0], qz.at[d], z_peer(d)) for d in z_steps]

    wanted_z = jnp.zeros((2 * a_len, HEAD_DIM), jnp.int32) + anchor_z
    chosen = a2[0].astype(F32)
    for d in z_steps:
        a2_in[d].wait_recv()
        origin = lax.rem(z + NZ - d, NZ)
        chosen = jnp.where(wanted_z == origin, a2[d].astype(F32), chosen)
    anc[p] = chosen.astype(BF16)
    a3_in = [send(anc.at[p], anc.at[p], p_peer(dy, dc)) for dy, dc in p_steps]

    query = acc[:, :QCOLS] + dot_nn(tok[3, 2], w_in[3, last_rows, :QCOLS])
    for h in range(HEADS):
        head = query[:, h * HEAD_DIM:(h + 1) * HEAD_DIM]
        q4[h * BLK:(h + 1) * BLK] = rotate(head, cosine, sine).astype(BF16)
    key_at = lax.broadcasted_iota(jnp.int32, (HEADS * BLK, BLK), 1)
    query_at = lax.rem(lax.broadcasted_iota(jnp.int32, (HEADS * BLK, BLK), 0), BLK)
    seen = (key_at <= query_at) & (key_at < lengths_s[c])
    scores = jnp.where(seen, dot_nt(q4[...], kvb[0, 0, :BLK]) * SCALE, NEG_BIG)
    own_max = jnp.max(scores, axis=1, keepdims=True)
    weights = jnp.where(seen, jnp.exp(scores - own_max), 0.0)
    own_sum = jnp.sum(weights, axis=1, keepdims=True)
    own_value = dot_nn(weights.astype(BF16), kvb[0, 0, BLK:])

    for copy in kv_in:
        copy.wait_recv()
    sib_in = send(kvb.at[0], kvb.at[1], (at(y, z, 1 - core), g)) if NC > 1 else None

    done = len(copies) - len(a3_in) - 1
    for copy in copies[:done]:
        copy.wait_send()

    for copy in a3_in:
        copy.wait_recv()
    a_keys = anc[:, :a_len].reshape(BLK, HEAD_DIM)
    a_values = anc[:, a_len:].reshape(BLK, HEAD_DIM)
    far = (key_at < lengths_s[anchor_block]) & (jnp.zeros_like(key_at) + anchor_block != c)
    scores = jnp.where(far, dot_nt(q4[...], a_keys) * SCALE, NEG_BIG)
    row_max = jnp.maximum(own_max, jnp.max(scores, axis=1, keepdims=True))
    weights = jnp.where(far, jnp.exp(scores - row_max), 0.0)
    own_factor = jnp.exp(own_max - row_max)
    total = jnp.sum(weights, axis=1, keepdims=True) + own_sum * own_factor
    value = dot_nn(weights.astype(BF16), a_values) + own_value * own_factor
    value = (value / total).astype(BF16)
    attended = jnp.concatenate([value[h * BLK:(h + 1) * BLK] for h in range(HEADS)], axis=1)

    def term(slot, j):
        return dot_nn(attended, w_out[slot, :, j * quarter:(j + 1) * quarter])

    wo_loads[3].wait()
    tr = {}
    for j in (0, 3, 1, 2):
        tr_out[j] = term(3, j).astype(BF16)
        tr[j] = send(tr_out.at[j], tr_in.at[j], right if j < 2 else left)
    for copy in qz_in:
        copy.wait_recv()
    queries = qz[...].reshape(n_q, HEAD_DIM)
    if sib_in is not None:
        sib_in.wait_recv()
    blocks = []
    key_row = lax.broadcasted_iota(jnp.int32, (BLK, n_q), 0)
    part_max = jnp.full((1, n_q), NEG_BIG, F32)
    for k in range(NC):
        for d in range(NY):
            number = at(lax.rem(y + NY - d, NY), z, flip(k))
            visible = (key_row < lengths_s[number]) & (key_row + number * BLK <= reach)
            block_scores = dot_nt(kvb[k, d, :BLK], queries) * SCALE
            block_scores = jnp.where(visible, block_scores, NEG_BIG)
            part_max = jnp.maximum(part_max, jnp.max(block_scores, axis=0, keepdims=True))
            blocks.append((k, d, visible, block_scores))
    part_sum = jnp.zeros((1, n_q), F32)
    part_value = jnp.zeros((n_q, HEAD_DIM), F32)
    for k, d, visible, block_scores in blocks:
        block_weights = jnp.where(visible, jnp.exp(block_scores - part_max), 0.0)
        part_sum = part_sum + jnp.sum(block_weights, axis=0, keepdims=True)
        part_value = part_value + dot_tn(block_weights.astype(BF16), kvb[k, d, BLK:])
    n_r = HEADS * QROW
    stats = jnp.concatenate(
        split3(part_max) + split3(part_sum) + [jnp.zeros((10, n_q), F32)], axis=0
    ).astype(BF16)
    if n_q < LANES:
        stats = jnp.concatenate([stats, jnp.zeros((16, LANES - n_q), BF16)], axis=1)
    part[:, :n_r] = part_value.astype(BF16).reshape(NZ, n_r, HEAD_DIM)
    for d in range(NZ):
        group = d * n_r // LANES * LANES
        part[d, n_r:] = stats[:, group:group + LANES]
    part_ins = {NZ - d: send(part.at[d], part_in.at[NZ - d], z_peer(NZ - d)) for d in z_steps}

    wo_loads[2].wait()
    wo_loads[1].wait()
    final_r, final_l = {}, {}
    for j in (2, 3):
        to_right[j] = term(2, j).astype(BF16)
        final_r[j] = send(to_right.at[j], from_left.at[j], right)
        i = 3 - j
        to_left[i] = term(1, i).astype(BF16)
        final_l[i] = send(to_left.at[i], from_right.at[i], left)
    r_terms = {j: term(2, j) for j in (0, 1)}
    l_terms = {j: term(1, j) for j in (3, 2)}

    for j in (0, 1):
        tr[j].wait_recv()
        to_right[j] = (r_terms[j] + tr_in[j].astype(F32)).astype(BF16)
        final_r[j] = send(to_right.at[j], from_left.at[j], right)
        i = 3 - j
        tr[i].wait_recv()
        to_left[i] = (l_terms[i] + tr_in[i].astype(F32)).astype(BF16)
        final_l[i] = send(to_left.at[i], from_right.at[i], left)
    eye_row = lax.broadcasted_iota(jnp.int32, (n_r, LANES), 0)
    eye_lane = lax.broadcasted_iota(jnp.int32, (n_r, LANES), 1)

    def column(rows, first, slot):
        line = rows[first:first + 1] + rows[first + 1:first + 2] + rows[first + 2:first + 3]
        spot = eye_lane == eye_row + (slot * n_r) % LANES
        return jnp.sum(jnp.where(spot, line, 0.0), axis=1, keepdims=True)

    maxima, sums, values = [], [], []
    for d in range(NZ):
        if d:
            part_ins[d].wait_recv()
        block = (part_in[d] if d else part[0]).astype(F32)
        slot = (NZ - d) % NZ
        maxima.append(column(block[n_r:], 0, slot))
        sums.append(column(block[n_r:], 3, slot))
        values.append(block[:n_r])
    top_max = maxima[0]
    for one in maxima[1:]:
        top_max = jnp.maximum(top_max, one)
    all_sum = jnp.zeros((n_r, 1), F32)
    all_value = jnp.zeros((n_r, HEAD_DIM), F32)
    for one_max, one_sum, one_value in zip(maxima, sums, values):
        factor = jnp.exp(one_max - top_max)
        all_sum = all_sum + one_sum * factor
        all_value = all_value + one_value * factor
    all_value = all_value / all_sum
    q_att = jnp.concatenate([all_value[h * QROW:(h + 1) * QROW] for h in range(HEADS)], axis=1)
    q_att = jnp.concatenate([q_att, jnp.zeros_like(q_att)], axis=0).astype(BF16)
    qx_in_copies = []
    for slot, device in ((3, opposite), (2, right), (1, left)):
        q_term = dot_nn(q_att, w_out[slot])[:QROW]
        qx_out[slot] = jnp.concatenate([q_term[:, :half_f], q_term[:, half_f:]], axis=0).astype(BF16)
        qx_in_copies.append(send(qx_out.at[slot], qx_in.at[slot], device))
    wo_loads[0].wait()
    q_own = dot_nn(q_att, w_out[0])[:QROW]

    own_term[...] = dot_nn(attended, w_out[0])

    for j in (2, 1, 0, 3):
        final_r[j].wait_recv()
        final_l[j].wait_recv()
        columns = slice(j * quarter, (j + 1) * quarter)
        ctx_out[:, columns] = (
            own_term[:, columns] + from_left[j].astype(F32) + from_right[j].astype(F32)
        ).astype(BF16)
    for copy in qx_in_copies:
        copy.wait_recv()
    for slot in (1, 2, 3):
        packed = qx_in[slot].astype(F32)
        q_own = q_own + jnp.concatenate([packed[:QROW], packed[QROW:]], axis=1)
    q_out[...] = q_own.astype(BF16)
    for copy in copies[done:]:
        copy.wait_send()


def split3(x):
    high = x.astype(BF16).astype(F32)
    middle = (x - high).astype(BF16).astype(F32)
    return [high, middle, x - high - middle]


def local(tokens, questions, q_weight, k_weight, v_weight, o_weight, anchor, lengths, positions):
    n_r = HEADS * QROW
    n_p = NY * NC
    a_len = BLK // n_p
    anywhere = pl.BlockSpec(memory_space=pltpu.HBM)
    vmem = pl.BlockSpec(memory_space=pltpu.VMEM)
    smem = pl.BlockSpec(memory_space=pltpu.SMEM)
    operands = [
        pltpu.with_memory_space_constraint(x, pltpu.HBM)
        for x in (tokens, questions, q_weight, k_weight, v_weight, o_weight)
    ]
    lengths, positions = [
        pltpu.with_memory_space_constraint(x, pltpu.HBM) for x in (lengths, positions)
    ]
    return pl.pallas_call(
        kernel,
        out_shape=(
            jax.ShapeDtypeStruct((BLK, FEAT), BF16),
            jax.ShapeDtypeStruct((QROW, FEAT), BF16),
        ),
        in_specs=[anywhere] * 6 + [smem] + [anywhere] * 2,
        out_specs=(vmem, vmem),
        scratch_shapes=[
            pltpu.VMEM((QROW, FEAT), BF16),
            pltpu.SMEM(lengths.shape, jnp.int32),
            pltpu.SMEM(positions.shape, jnp.int32),
            pltpu.VMEM((NX, FEAT, WCOLS), BF16),
            pltpu.VMEM((NX, QCOLS, FEAT), BF16),
            pltpu.VMEM((BLK, FEAT), BF16),
            pltpu.VMEM((NX, 4, BLK, FEAT // 4), BF16),
            pltpu.VMEM((NX, 2 * QROW, FEAT // 2), BF16),
            pltpu.VMEM((BLK, WCOLS), F32),
            pltpu.VMEM((HEADS * BLK, HEAD_DIM), BF16),
            pltpu.VMEM((NZ, n_r, HEAD_DIM), BF16),
            pltpu.VMEM((NC, NY, 2 * BLK, HEAD_DIM), BF16),
            pltpu.VMEM((n_p, a_len, FEAT), BF16),
            pltpu.VMEM((NX, a_len, FEAT), BF16),
            pltpu.VMEM((NZ, 2 * a_len, HEAD_DIM), BF16),
            pltpu.VMEM((n_p, 2 * a_len, HEAD_DIM), BF16),
            pltpu.VMEM((NZ, n_r + 16, HEAD_DIM), BF16),
            pltpu.VMEM((NZ, n_r + 16, HEAD_DIM), BF16),
            pltpu.VMEM((4, BLK, FEAT // 4), BF16),
            pltpu.VMEM((4, BLK, FEAT // 4), BF16),
            pltpu.VMEM((4, BLK, FEAT // 4), BF16),
            pltpu.VMEM((4, BLK, FEAT // 4), BF16),
            pltpu.VMEM((4, BLK, FEAT // 4), BF16),
            pltpu.VMEM((4, BLK, FEAT // 4), BF16),
            pltpu.VMEM((BLK, FEAT), F32),
            pltpu.VMEM((NX, 2 * QROW, FEAT // 2), BF16),
            pltpu.VMEM((NX, 2 * QROW, FEAT // 2), BF16),
            pltpu.SemaphoreType.DMA((N_LOADS,)),
            pltpu.SemaphoreType.DMA((N_COPIES,)),
            pltpu.SemaphoreType.DMA((N_COPIES,)),
        ],
        compiler_params=pltpu.CompilerParams(
            collective_id=0, has_side_effects=True, vmem_limit_bytes=40 * 2**20
        ),
        name="fused_attention",
    )(*operands, anchor, lengths, positions)


def solution(mesh):
    in_specs = (
        P("ctx", "kvg"),
        P("ctx", "kvg"),
        P(None, "kvg"),
        P(None, "kvg"),
        P(None, "kvg"),
        P("kvg", None),
        P(),
        P(),
        P(),
    )
    out_specs = (P("ctx", "kvg"), P("ctx", "kvg"))
    return jax.shard_map(local, mesh=mesh, in_specs=in_specs, out_specs=out_specs, check_vma=False)
```

```python
import math

import jax
import jax.numpy as jnp
from jax import lax
from jax.experimental import pallas as pl
from jax.experimental.pallas import tpu as pltpu
from jax.sharding import PartitionSpec as P

HEAD_DIM = 128
NX = 4
NY, NZ, NC = 4, 8, 2
BLK = 128
QROW = 8
HEADS = 4
FEAT = 1024
QCOLS = HEADS * HEAD_DIM
WCOLS = QCOLS + 2 * HEAD_DIM
NEG_BIG = -1e30
SCALE = HEAD_DIM ** (-0.5)
F32 = jnp.float32
BF16 = jnp.bfloat16
MESH = pl.DeviceIdType.MESH
LANES = 128
N_COPIES = 96
N_LOADS = 20


def dot_nn(a, b):
    return jnp.dot(a, b, preferred_element_type=F32)


def dot_nt(a, b):
    return lax.dot_general(a, b, (((1,), (1,)), ((), ())), preferred_element_type=F32)


def dot_tn(a, b):
    return lax.dot_general(a, b, (((0,), (0,)), ((), ())), preferred_element_type=F32)


def angles(places):
    lane = lax.broadcasted_iota(jnp.int32, places.shape, 1)
    half = HEAD_DIM // 2
    index = jnp.where(lane < half, lane, lane - half).astype(F32)
    frequency = jnp.exp(index * (-2.0 * math.log(500000.0) / HEAD_DIM))
    angle = places.astype(F32) * frequency
    sine = jnp.sin(angle)
    return jnp.cos(angle), jnp.where(lane < half, -sine, sine)


def rotate(head, cosine, sine):
    return head * cosine + pltpu.roll(head, HEAD_DIM // 2, 1) * sine


def kernel(
    tokens, questions, wq, wk, wv, wo, anchor, lengths, positions,
    ctx_out, q_out,
    asked, lengths_s, positions_s, w_in, w_out, own_tok, tok, qpack, acc, q4, qz, kvb,
    a_rows, a_tok, a2, anc, part, part_in, tr_out, tr_in, to_right, to_left,
    from_left, from_right, own_term, qx_out, qx_in, load_sem, send_sem, recv_sem,
):
    n_p = NY * NC
    a_len = BLK // n_p
    c = lax.axis_index("ctx")
    g = lax.axis_index("kvg")
    core = lax.rem(c, NC)
    z = lax.rem(lax.div(c, NC), NZ)
    y = lax.div(c, NC * NZ)
    p = y * NC + core

    def at(y_, z_, core_):
        return (y_ * NZ + z_) * NC + core_

    src = [g, lax.rem(g + 3, NX), lax.rem(g + 1, NX), lax.rem(g + 2, NX)]
    left, right, opposite = (c, src[1]), (c, src[2]), (c, src[3])

    def flip(dc):
        return 1 - core if dc else core

    p_steps = [(dy, dc) for dy in range(NY) for dc in range(NC) if dy or dc]
    p_steps.sort(key=lambda s: (-min(s[0], NY - s[0]), -s[1]))
    z_steps = sorted(range(1, NZ), key=lambda d: -min(d, NZ - d))

    def p_peer(dy, dc):
        return (at(lax.rem(y + dy, NY), z, flip(dc)), g)

    def p_index(dy, dc):
        return lax.rem(y + dy, NY) * NC + flip(dc)

    def z_peer(d):
        return (at(y, lax.rem(z + d, NZ), core), g)

    partners = [z_peer(d) for d in z_steps] + [opposite]
    partners += [p_peer(dy, dc) for dy, dc in p_steps] + [left, right]
    barrier = pltpu.get_barrier_semaphore()
    for partner in partners:
        pl.semaphore_signal(barrier, inc=1, device_id=partner, device_id_type=MESH)

    loads = []

    def load(source, target):
        copy = pltpu.make_async_copy(source, target, load_sem.at[len(loads)])
        copy.start()
        loads.append(copy)
        return copy

    asked_load = load(questions, asked)
    scalar_loads = [load(lengths, lengths_s), load(positions, positions_s)]
    tok_load = load(tokens, own_tok)
    w_loads = []
    for slot in range(NX):
        rows = pl.ds(pl.multiple_of(src[slot] * FEAT, FEAT), FEAT)
        w_loads.append([
            load(wq.at[rows, :], w_in.at[slot, :, pl.ds(0, QCOLS)]),
            load(wk.at[rows, :], w_in.at[slot, :, pl.ds(QCOLS, HEAD_DIM)]),
            load(wv.at[rows, :], w_in.at[slot, :, pl.ds(QCOLS + HEAD_DIM, HEAD_DIM)]),
        ])

    asked_load.wait()
    own_questions = asked[...].astype(F32)
    half_f = FEAT // 2
    qpack[0] = jnp.concatenate(
        [own_questions[:, :half_f], own_questions[:, half_f:]], axis=0
    ).astype(BF16)
    pl.semaphore_wait(barrier, len(partners))

    copies = []

    def send(source, target, device):
        index = len(copies)
        copy = pltpu.make_async_remote_copy(
            src_ref=source, dst_ref=target, send_sem=send_sem.at[index],
            recv_sem=recv_sem.at[index], device_id=device, device_id_type=MESH,
        )
        copy.start()
        copies.append(copy)
        return copy

    quarter = FEAT // 4
    near_r, near_l = {}, {}

    def send_tokens(j_r, j_l):
        near_r[j_r] = send(tokens.at[:, pl.ds(j_r * quarter, quarter)], tok.at[1, j_r], right)
        near_l[j_l] = send(tokens.at[:, pl.ds(j_l * quarter, quarter)], tok.at[2, j_l], left)

    send_tokens(0, 3)
    a_in = {}
    for dy, dc in p_steps:
        there = pl.ds(pl.multiple_of(p_index(dy, dc) * a_len, a_len), a_len)
        a_in[dy, dc] = send(tokens.at[there, :], a_rows.at[dy * NC + dc], p_peer(dy, dc))
    send_tokens(1, 2)

    tok_load.wait()
    for copy in w_loads[0]:
        copy.wait()
    acc[...] = dot_nn(own_tok[...], w_in[0])
    row = lax.broadcasted_iota(jnp.int32, (BLK, HEAD_DIM), 0)
    cosine, sine = angles(row + c * BLK)
    send_tokens(2, 1)
    for copy in scalar_loads:
        copy.wait()
    q_row = lax.broadcasted_iota(jnp.int32, (QROW, HEAD_DIM), 0)
    q_places = jnp.zeros((QROW, HEAD_DIM), jnp.int32)
    for r in range(QROW):
        q_places = jnp.where(q_row == r, positions_s[c * QROW + r], q_places)
    q_cosine, q_sine = angles(q_places)
    anchor_block = anchor[0]
    anchor_y = lax.div(anchor_block, NC * NZ)
    anchor_core = lax.rem(anchor_block, NC)
    anchor_z = lax.rem(lax.div(anchor_block, NC), NZ)
    a_row = lax.broadcasted_iota(jnp.int32, (a_len, HEAD_DIM), 0)
    a_cosine, a_sine = angles(a_row + p * a_len + anchor_block * BLK)

    n_q = NZ * HEADS * QROW
    lane = lax.broadcasted_iota(jnp.int32, (1, n_q), 1)
    reach = jnp.zeros((1, n_q), jnp.int32)
    for d in range(NZ):
        there = at(y, lax.rem(z + NZ - d, NZ), core) * QROW
        for r in range(QROW):
            spot = (lax.div(lane, HEADS * QROW) == d) & (lax.rem(lane, QROW) == r)
            reach = jnp.where(spot, positions_s[there + r], reach)

    wanted = jnp.zeros((a_len, FEAT), jnp.int32)
    wanted_p = wanted + (anchor_y * NC + anchor_core)
    chosen = own_tok[pl.ds(pl.multiple_of(p * a_len, a_len), a_len), :].astype(F32)
    for dy, dc in p_steps:
        a_in[dy, dc].wait_recv()
        origin = lax.rem(y + NY - dy, NY) * NC + flip(dc)
        chosen = jnp.where(wanted_p == origin, a_rows[dy * NC + dc].astype(F32), chosen)
    a_tok[0] = chosen.astype(BF16)
    at_in = [
        send(a_tok.at[0], a_tok.at[3], opposite),
        send(a_tok.at[0], a_tok.at[1], right),
        send(a_tok.at[0], a_tok.at[2], left),
    ]

    send_tokens(3, 0)

    far_r, far_l = {}, {}

    def pass_on(j_r, j_l):
        near_r[j_r].wait_recv()
        far_r[j_r] = send(tok.at[1, j_r], tok.at[3, j_r], right)
        near_l[j_l].wait_recv()
        far_l[j_l] = send(tok.at[2, j_l], tok.at[3, j_l], left)

    pass_on(0, 3)
    pass_on(1, 2)
    q_in = [
        send(qpack.at[0], qpack.at[3], opposite),
        send(qpack.at[0], qpack.at[1], right),
        send(qpack.at[0], qpack.at[2], left),
    ]

    for slot in (1, 2):
        for copy in w_loads[slot]:
            copy.wait()
    for j in range(2):
        acc[...] += dot_nn(tok[1, j], w_in[1, j * quarter:(j + 1) * quarter])
        k = 3 - j
        acc[...] += dot_nn(tok[2, k], w_in[2, k * quarter:(k + 1) * quarter])
    for copy in w_loads[3]:
        copy.wait()
    for copy in at_in:
        copy.wait_recv()
    a_kv = jnp.zeros((a_len, 2 * HEAD_DIM), F32)
    for slot in range(NX):
        a_kv = a_kv + dot_nn(a_tok[slot], w_in[slot, :, QCOLS:])
    a2[0, :a_len] = rotate(a_kv[:, :HEAD_DIM], a_cosine, a_sine).astype(BF16)
    a2[0, a_len:] = a_kv[:, HEAD_DIM:].astype(BF16)
    a2_in = {d: send(a2.at[0], a2.at[d], z_peer(d)) for d in z_steps}
    wo_loads = {}
    for slot in (3, 2, 1, 0):
        columns = pl.ds(pl.multiple_of(src[slot] * FEAT, FEAT), FEAT)
        wo_loads[slot] = load(wo.at[:, columns], w_out.at[slot])

    for j in range(2, 4):
        near_r[j].wait_recv()
        acc[...] += dot_nn(tok[1, j], w_in[1, j * quarter:(j + 1) * quarter])
        k = 3 - j
        near_l[k].wait_recv()
        acc[...] += dot_nn(tok[2, k], w_in[2, k * quarter:(k + 1) * quarter])

    for j in (0, 3, 1):
        (far_r if j < 2 else far_l)[j].wait_recv()
        acc[...] += dot_nn(tok[3, j], w_in[3, j * quarter:(j + 1) * quarter])
    far_l[2].wait_recv()
    last_rows = slice(2 * quarter, 3 * quarter)
    key_value = acc[:, QCOLS:] + dot_nn(tok[3, 2], w_in[3, last_rows, QCOLS:])
    kvb[0, 0, :BLK] = rotate(key_value[:, :HEAD_DIM], cosine, sine).astype(BF16)
    kvb[0, 0, BLK:] = key_value[:, HEAD_DIM:].astype(BF16)
    kv_in = [
        send(kvb.at[0, 0], kvb.at[0, d], p_peer(d, 0))
        for d in sorted(range(1, NY), key=lambda d: -min(d, NY - d))
    ]
    sibling = (at(y, z, 1 - core), g)
    sib_own = send(kvb.at[0, 0], kvb.at[1, 0], sibling)

    for copy in q_in:
        copy.wait_recv()
    q_total = jnp.zeros((2 * QROW, QCOLS), F32)
    for slot in range(NX):
        packed = qpack[slot].astype(F32)
        rows = jnp.concatenate([packed[:QROW], packed[QROW:]], axis=1)
        rows = jnp.concatenate([rows, jnp.zeros_like(rows)], axis=0).astype(BF16)
        q_total = q_total + dot_nn(rows, w_in[slot, :, :QCOLS])
    q_heads = [
        rotate(q_total[:QROW, h * HEAD_DIM:(h + 1) * HEAD_DIM], q_cosine, q_sine)
        for h in range(HEADS)
    ]
    qz[0] = jnp.concatenate(q_heads, axis=0).astype(BF16)
    qz_in = [send(qz.at[0], qz.at[d], z_peer(d)) for d in z_steps]

    wanted_z = jnp.zeros((2 * a_len, HEAD_DIM), jnp.int32) + anchor_z
    chosen = a2[0].astype(F32)
    for d in z_steps:
        a2_in[d].wait_recv()
        origin = lax.rem(z + NZ - d, NZ)
        chosen = jnp.where(wanted_z == origin, a2[d].astype(F32), chosen)
    anc[p] = chosen.astype(BF16)
    a3_in = [send(anc.at[p], anc.at[p], p_peer(dy, dc)) for dy, dc in p_steps]

    query = acc[:, :QCOLS] + dot_nn(tok[3, 2], w_in[3, last_rows, :QCOLS])
    for h in range(HEADS):
        head = query[:, h * HEAD_DIM:(h + 1) * HEAD_DIM]
        q4[h * BLK:(h + 1) * BLK] = rotate(head, cosine, sine).astype(BF16)
    key_at = lax.broadcasted_iota(jnp.int32, (HEADS * BLK, BLK), 1)
    query_at = lax.rem(lax.broadcasted_iota(jnp.int32, (HEADS * BLK, BLK), 0), BLK)
    seen = (key_at <= query_at) & (key_at < lengths_s[c])
    scores = jnp.where(seen, dot_nt(q4[...], kvb[0, 0, :BLK]) * SCALE, NEG_BIG)
    own_max = jnp.max(scores, axis=1, keepdims=True)
    weights = jnp.where(seen, jnp.exp(scores - own_max), 0.0)
    own_sum = jnp.sum(weights, axis=1, keepdims=True)
    own_value = dot_nn(weights.astype(BF16), kvb[0, 0, BLK:])

    for copy in qz_in:
        copy.wait_recv()
    for copy in kv_in:
        copy.wait_recv()
    rest = pl.ds(1, NY - 1)
    sib_in = send(kvb.at[0, rest], kvb.at[1, rest], sibling)

    done = len(copies) - len(a3_in) - 1
    for copy in copies[:done]:
        copy.wait_send()

    for copy in a3_in:
        copy.wait_recv()
    a_keys = anc[:, :a_len].reshape(BLK, HEAD_DIM)
    a_values = anc[:, a_len:].reshape(BLK, HEAD_DIM)
    far = (key_at < lengths_s[anchor_block]) & (jnp.zeros_like(key_at) + anchor_block != c)
    scores = jnp.where(far, dot_nt(q4[...], a_keys) * SCALE, NEG_BIG)
    row_max = jnp.maximum(own_max, jnp.max(scores, axis=1, keepdims=True))
    weights = jnp.where(far, jnp.exp(scores - row_max), 0.0)
    own_factor = jnp.exp(own_max - row_max)
    total = jnp.sum(weights, axis=1, keepdims=True) + own_sum * own_factor
    value = dot_nn(weights.astype(BF16), a_values) + own_value * own_factor
    value = (value / total).astype(BF16)
    attended = jnp.concatenate([value[h * BLK:(h + 1) * BLK] for h in range(HEADS)], axis=1)

    def term(slot, j):
        return dot_nn(attended, w_out[slot, :, j * quarter:(j + 1) * quarter])

    wo_loads[3].wait()
    tr = {}
    for j in (0, 3, 1, 2):
        tr_out[j] = term(3, j).astype(BF16)
        tr[j] = send(tr_out.at[j], tr_in.at[j], right if j < 2 else left)
    queries = qz[...].reshape(n_q, HEAD_DIM)
    sib_own.wait_recv()
    sib_in.wait_recv()
    blocks = []
    key_row = lax.broadcasted_iota(jnp.int32, (BLK, n_q), 0)
    part_max = jnp.full((1, n_q), NEG_BIG, F32)
    for k in range(NC):
        for d in range(NY):
            number = at(lax.rem(y + NY - d, NY), z, flip(k))
            visible = (key_row < lengths_s[number]) & (key_row + number * BLK <= reach)
            block_scores = dot_nt(kvb[k, d, :BLK], queries) * SCALE
            block_scores = jnp.where(visible, block_scores, NEG_BIG)
            part_max = jnp.maximum(part_max, jnp.max(block_scores, axis=0, keepdims=True))
            blocks.append((k, d, visible, block_scores))
    part_sum = jnp.zeros((1, n_q), F32)
    part_value = jnp.zeros((n_q, HEAD_DIM), F32)
    for k, d, visible, block_scores in blocks:
        block_weights = jnp.where(visible, jnp.exp(block_scores - part_max), 0.0)
        part_sum = part_sum + jnp.sum(block_weights, axis=0, keepdims=True)
        part_value = part_value + dot_tn(block_weights.astype(BF16), kvb[k, d, BLK:])
    n_r = HEADS * QROW
    stats = jnp.concatenate(
        split3(part_max) + split3(part_sum) + [jnp.zeros((10, n_q), F32)], axis=0
    ).astype(BF16)
    if n_q < LANES:
        stats = jnp.concatenate([stats, jnp.zeros((16, LANES - n_q), BF16)], axis=1)
    part[:, :n_r] = part_value.astype(BF16).reshape(NZ, n_r, HEAD_DIM)
    for d in range(NZ):
        group = d * n_r // LANES * LANES
        part[d, n_r:] = stats[:, group:group + LANES]
    part_ins = {NZ - d: send(part.at[d], part_in.at[NZ - d], z_peer(NZ - d)) for d in z_steps}

    wo_loads[2].wait()
    wo_loads[1].wait()
    final_r, final_l = {}, {}
    for j in (2, 3):
        to_right[j] = term(2, j).astype(BF16)
        final_r[j] = send(to_right.at[j], from_left.at[j], right)
        i = 3 - j
        to_left[i] = term(1, i).astype(BF16)
        final_l[i] = send(to_left.at[i], from_right.at[i], left)
    r_terms = {j: term(2, j) for j in (0, 1)}
    l_terms = {j: term(1, j) for j in (3, 2)}

    for j in (0, 1):
        tr[j].wait_recv()
        to_right[j] = (r_terms[j] + tr_in[j].astype(F32)).astype(BF16)
        final_r[j] = send(to_right.at[j], from_left.at[j], right)
        i = 3 - j
        tr[i].wait_recv()
        to_left[i] = (l_terms[i] + tr_in[i].astype(F32)).astype(BF16)
        final_l[i] = send(to_left.at[i], from_right.at[i], left)
    eye_row = lax.broadcasted_iota(jnp.int32, (n_r, LANES), 0)
    eye_lane = lax.broadcasted_iota(jnp.int32, (n_r, LANES), 1)

    def column(rows, first, slot):
        line = rows[first:first + 1] + rows[first + 1:first + 2] + rows[first + 2:first + 3]
        spot = eye_lane == eye_row + (slot * n_r) % LANES
        return jnp.sum(jnp.where(spot, line, 0.0), axis=1, keepdims=True)

    maxima, sums, values = [], [], []
    for d in range(NZ):
        if d:
            part_ins[d].wait_recv()
        block = (part_in[d] if d else part[0]).astype(F32)
        slot = (NZ - d) % NZ
        maxima.append(column(block[n_r:], 0, slot))
        sums.append(column(block[n_r:], 3, slot))
        values.append(block[:n_r])
    top_max = maxima[0]
    for one in maxima[1:]:
        top_max = jnp.maximum(top_max, one)
    all_sum = jnp.zeros((n_r, 1), F32)
    all_value = jnp.zeros((n_r, HEAD_DIM), F32)
    for one_max, one_sum, one_value in zip(maxima, sums, values):
        factor = jnp.exp(one_max - top_max)
        all_sum = all_sum + one_sum * factor
        all_value = all_value + one_value * factor
    all_value = all_value / all_sum
    q_att = jnp.concatenate([all_value[h * QROW:(h + 1) * QROW] for h in range(HEADS)], axis=1)
    q_att = jnp.concatenate([q_att, jnp.zeros_like(q_att)], axis=0).astype(BF16)
    qx_in_copies = []
    for slot, device in ((3, opposite), (2, right), (1, left)):
        q_term = dot_nn(q_att, w_out[slot])[:QROW]
        qx_out[slot] = jnp.concatenate([q_term[:, :half_f], q_term[:, half_f:]], axis=0).astype(BF16)
        qx_in_copies.append(send(qx_out.at[slot], qx_in.at[slot], device))
    wo_loads[0].wait()
    q_own = dot_nn(q_att, w_out[0])[:QROW]

    own_term[...] = dot_nn(attended, w_out[0])

    for j in (2, 1, 0, 3):
        final_r[j].wait_recv()
        final_l[j].wait_recv()
        columns = slice(j * quarter, (j + 1) * quarter)
        ctx_out[:, columns] = (
            own_term[:, columns] + from_left[j].astype(F32) + from_right[j].astype(F32)
        ).astype(BF16)
    for copy in qx_in_copies:
        copy.wait_recv()
    for slot in (1, 2, 3):
        packed = qx_in[slot].astype(F32)
        q_own = q_own + jnp.concatenate([packed[:QROW], packed[QROW:]], axis=1)
    q_out[...] = q_own.astype(BF16)
    for copy in copies[done:]:
        copy.wait_send()


def split3(x):
    high = x.astype(BF16).astype(F32)
    middle = (x - high).astype(BF16).astype(F32)
    return [high, middle, x - high - middle]


def local(tokens, questions, q_weight, k_weight, v_weight, o_weight, anchor, lengths, positions):
    n_r = HEADS * QROW
    n_p = NY * NC
    a_len = BLK // n_p
    anywhere = pl.BlockSpec(memory_space=pltpu.HBM)
    vmem = pl.BlockSpec(memory_space=pltpu.VMEM)
    smem = pl.BlockSpec(memory_space=pltpu.SMEM)
    operands = [
        pltpu.with_memory_space_constraint(x, pltpu.HBM)
        for x in (tokens, questions, q_weight, k_weight, v_weight, o_weight)
    ]
    lengths, positions = [
        pltpu.with_memory_space_constraint(x, pltpu.HBM) for x in (lengths, positions)
    ]
    return pl.pallas_call(
        kernel,
        out_shape=(
            jax.ShapeDtypeStruct((BLK, FEAT), BF16),
            jax.ShapeDtypeStruct((QROW, FEAT), BF16),
        ),
        in_specs=[anywhere] * 6 + [smem] + [anywhere] * 2,
        out_specs=(vmem, vmem),
        scratch_shapes=[
            pltpu.VMEM((QROW, FEAT), BF16),
            pltpu.SMEM(lengths.shape, jnp.int32),
            pltpu.SMEM(positions.shape, jnp.int32),
            pltpu.VMEM((NX, FEAT, WCOLS), BF16),
            pltpu.VMEM((NX, QCOLS, FEAT), BF16),
            pltpu.VMEM((BLK, FEAT), BF16),
            pltpu.VMEM((NX, 4, BLK, FEAT // 4), BF16),
            pltpu.VMEM((NX, 2 * QROW, FEAT // 2), BF16),
            pltpu.VMEM((BLK, WCOLS), F32),
            pltpu.VMEM((HEADS * BLK, HEAD_DIM), BF16),
            pltpu.VMEM((NZ, n_r, HEAD_DIM), BF16),
            pltpu.VMEM((NC, NY, 2 * BLK, HEAD_DIM), BF16),
            pltpu.VMEM((n_p, a_len, FEAT), BF16),
            pltpu.VMEM((NX, a_len, FEAT), BF16),
            pltpu.VMEM((NZ, 2 * a_len, HEAD_DIM), BF16),
            pltpu.VMEM((n_p, 2 * a_len, HEAD_DIM), BF16),
            pltpu.VMEM((NZ, n_r + 16, HEAD_DIM), BF16),
            pltpu.VMEM((NZ, n_r + 16, HEAD_DIM), BF16),
            pltpu.VMEM((4, BLK, FEAT // 4), BF16),
            pltpu.VMEM((4, BLK, FEAT // 4), BF16),
            pltpu.VMEM((4, BLK, FEAT // 4), BF16),
            pltpu.VMEM((4, BLK, FEAT // 4), BF16),
            pltpu.VMEM((4, BLK, FEAT // 4), BF16),
            pltpu.VMEM((4, BLK, FEAT // 4), BF16),
            pltpu.VMEM((BLK, FEAT), F32),
            pltpu.VMEM((NX, 2 * QROW, FEAT // 2), BF16),
            pltpu.VMEM((NX, 2 * QROW, FEAT // 2), BF16),
            pltpu.SemaphoreType.DMA((N_LOADS,)),
            pltpu.SemaphoreType.DMA((N_COPIES,)),
            pltpu.SemaphoreType.DMA((N_COPIES,)),
        ],
        compiler_params=pltpu.CompilerParams(
            collective_id=0, has_side_effects=True, vmem_limit_bytes=40 * 2**20
        ),
        name="fused_attention",
    )(*operands, anchor, lengths, positions)


def solution(mesh):
    in_specs = (
        P("ctx", "kvg"),
        P("ctx", "kvg"),
        P(None, "kvg"),
        P(None, "kvg"),
        P(None, "kvg"),
        P("kvg", None),
        P(),
        P(),
        P(),
    )
    out_specs = (P("ctx", "kvg"), P("ctx", "kvg"))
    return jax.shard_map(local, mesh=mesh, in_specs=in_specs, out_specs=out_specs, check_vma=False)
```
